512 devices in a mesh: tp: 32 (over z, y_hi), rep: 16 (over y_lo, x, core).
Axes of the slice: x: 4, y: 8 (y_hi: 4, y_lo: 2; y = y_hi * 2 + y_lo), z: 8, core: 2. Of those that a mesh axis runs over, the one named last changes fastest.
Arguments:
- tokens: bfloat16 [6144, 8192], P('rep', 'tp'), may hold values from -6 to 6
- row_lengths: int32 [32], P('rep'), may hold values from 1 to 192
- attn_gain: float32 [8192], P('tp'), may hold values from 0.1 to 1.9
- query_weight: bfloat16 [8192, 4096], P('rep', 'tp'), may hold values from -2 to 2
- key_weight: bfloat16 [8192, 512], P('rep', 'tp'), may hold values from -2 to 2
- value_matrix: bfloat16 [8192, 512], P('rep', 'tp'), may hold values from -0.0625 to 0.0625
- output_weight: bfloat16 [4096, 8192], P('rep', 'tp'), may hold values from -0.09375 to 0.09375
- final_gain: float32 [8192], P('tp'), may hold values from 0.1 to 1.9
- value_head: float32 [8192, 6], P('tp'), may hold values from -0.0625 to 0.0625
Outputs:
- resid_out: bfloat16 [6144, 8192], P('rep', 'tp')
- objective_scores: float32 [6144, 6], P('rep')
The draws below stay inside these ranges and needn't reach their ends.
All inputs are finite; a program needn't handle non-finite values.
Results may differ from the reference program's by a relative error of at most 0.025.
Values may be sent and summed in bfloat16 or wider, within the bound.
No kernel may reach another device: no remote copies, remote signals or barrier semaphores. Data moves between devices by JAX's collectives and lax.ppermute only.
A program may use at most 64 MiB of HBM per device.

```python
import math
import jax
import jax.numpy as jnp
from jax import lax

MODEL_WIDTH = 8192
QUERY_HEADS = 32
KEY_VALUE_HEADS = 4
HEAD_SIZE = 128
NOBJ = 6
ROW_LENGTH = 192
TOKENS = 6144
SEQS = 32


def shared_keys(key):
    return jax.random.normal(jax.random.fold_in(key, 11), (MODEL_WIDTH, KEY_VALUE_HEADS * HEAD_SIZE), jnp.float32) / math.sqrt(MODEL_WIDTH)


def draw_key_weight(key, part):
    return jnp.clip(shared_keys(key), -2.0, 2.0).astype(jnp.bfloat16)


def draw_query_weight(key, part):
    noise = jax.random.normal(jax.random.fold_in(key, 23), (MODEL_WIDTH, QUERY_HEADS * HEAD_SIZE), jnp.float32) / math.sqrt(MODEL_WIDTH)
    return jnp.clip(noise, -2.0, 2.0).astype(jnp.bfloat16)


def set_ends(array, stream_key, least, high):
    longest = array.shape.index(max(array.shape))
    spots = []
    for shift in (0, 1):
        where = [jax.random.randint(jax.random.fold_in(stream_key, axis), (), 0, length) for axis, length in enumerate(array.shape)]
        where[longest] = (where[longest] + shift) % array.shape[longest]
        spots.append(tuple(where))
    return array.at[spots[0]].set(least).at[spots[1]].set(high)


def shard_levels(stream_key, dims, cuts, smallest, high):
    def one(dim, shards_of):
        draws = jax.random.uniform(jax.random.fold_in(jax.random.fold_in(stream_key, 6), dim), (shards_of,), jnp.float32, smallest / len(cuts), high / len(cuts))
        return jnp.repeat(jnp.exp(draws), dims[dim] // shards_of).reshape((-1,) + (1,) * (len(dims) - dim - 1))

    factor_of = one(*cuts[0])
    for cut in cuts[1:]:
        factor_of = factor_of * one(*cut)
    return factor_of


def normal_values(rng, dims, width, reach, split=(), held_as=jnp.bfloat16):
    level = shard_levels(rng, dims, split, -0.22, 0.18) if split else 1.0
    values = jax.random.normal(rng, dims, jnp.float32) * width * level
    return jnp.minimum(jnp.maximum(values, -reach), reach).astype(held_as)


def setup_inputs(seed: int = 0) -> dict:
    key_list = jax.random.split(jax.random.key(seed), 10)
    return {
        "tokens": normal_values(key_list[0], (TOKENS, MODEL_WIDTH), 1.0, 6.0, ((0, 16), (1, 32))),
        "row_lengths": set_ends(jax.random.randint(key_list[1], (SEQS,), 1, ROW_LENGTH + 1), jax.random.fold_in(key_list[1], 1), 1, ROW_LENGTH).astype(jnp.int32),
        "attn_gain": jnp.clip(1.0 + 0.18 * jax.random.normal(key_list[2], (MODEL_WIDTH,), jnp.float32), 0.1, 1.9),
        "query_weight": draw_query_weight(jax.random.fold_in(key_list[9], 71), 0),
        "key_weight": draw_key_weight(jax.random.fold_in(key_list[9], 71), 0),
        "value_matrix": normal_values(key_list[5], (MODEL_WIDTH, KEY_VALUE_HEADS * HEAD_SIZE), MODEL_WIDTH ** -0.5, 0.0625, ((0, 16), (1, 32))),
        "output_weight": normal_values(key_list[6], (QUERY_HEADS * HEAD_SIZE, MODEL_WIDTH), (QUERY_HEADS * HEAD_SIZE) ** -0.5, 0.09375, ((0, 16), (1, 32))),
        "final_gain": jnp.clip(1.0 + 0.18 * jax.random.normal(key_list[7], (MODEL_WIDTH,), jnp.float32), 0.1, 1.9),
        "value_head": normal_values(key_list[8], (MODEL_WIDTH, NOBJ), MODEL_WIDTH ** -0.5, 0.0625, ((0, 32),), jnp.float32),
    }


EPS = 1e-05

def reference(tokens, row_lengths, attn_gain, query_weight, key_weight, value_matrix, output_weight, final_gain, value_head):
    xf = tokens.astype(jnp.float32)
    first_scale = lax.rsqrt(lax.optimization_barrier(jnp.mean(xf * xf, axis=1, keepdims=True)) + EPS)
    normed = (xf * first_scale * attn_gain).astype(jnp.bfloat16)
    query = jnp.dot(normed, query_weight, preferred_element_type=jnp.float32).astype(jnp.bfloat16)
    key_rows = jnp.dot(normed, key_weight, preferred_element_type=jnp.float32).astype(jnp.bfloat16)
    value_rows = jnp.dot(normed, value_matrix, preferred_element_type=jnp.float32).astype(jnp.bfloat16)
    every_row = tokens.shape[0] // ROW_LENGTH
    query4 = query.reshape(every_row, ROW_LENGTH, QUERY_HEADS, HEAD_SIZE)
    key_tensor4 = key_rows.reshape(every_row, ROW_LENGTH, KEY_VALUE_HEADS, HEAD_SIZE)
    value_tensor4 = value_rows.reshape(every_row, ROW_LENGTH, KEY_VALUE_HEADS, HEAD_SIZE)
    position = jnp.arange(ROW_LENGTH, dtype=jnp.int32)
    causal = position[None, :] <= position[:, None]
    allowed = causal[None, :, :] & (position[None, None, :] < row_lengths[:, None, None])
    inv_root = 1.0 / HEAD_SIZE ** 0.5

    def one_head(index):
        qpart = lax.dynamic_index_in_dim(query4, index, 2, keepdims=False).astype(jnp.float32)
        shared = (index % KEY_VALUE_HEADS).astype(jnp.int32)
        kpart = lax.dynamic_index_in_dim(key_tensor4, shared, 2, keepdims=False).astype(jnp.float32)
        vpart = lax.dynamic_index_in_dim(value_tensor4, shared, 2, keepdims=False).astype(jnp.float32)
        scores = jnp.einsum('rqd,rkd->rqk', qpart, kpart) * inv_root
        scores = jnp.where(allowed, scores, jnp.float32(-1e+30))
        scores = scores - lax.optimization_barrier(jnp.max(scores, axis=2, keepdims=True))
        expo = jnp.exp(scores)
        probs = (expo / lax.optimization_barrier(jnp.sum(expo, axis=2, keepdims=True))).astype(jnp.bfloat16)
        probs = lax.optimization_barrier(probs).astype(jnp.float32)
        return jnp.einsum('rqk,rkd->rqd', probs, vpart).astype(jnp.bfloat16)
    heads = lax.map(one_head, jnp.arange(QUERY_HEADS, dtype=jnp.int32))
    attended = jnp.transpose(heads, (1, 2, 0, 3)).reshape(tokens.shape[0], QUERY_HEADS * HEAD_SIZE)
    update = jnp.dot(attended, output_weight, preferred_element_type=jnp.float32)
    resid_out = (xf + update).astype(jnp.bfloat16)
    rfloat = resid_out.astype(jnp.float32)
    final_scale = lax.rsqrt(lax.optimization_barrier(jnp.mean(rfloat * rfloat, axis=1, keepdims=True)) + EPS)
    weighted = jnp.dot(rfloat * final_gain, value_head, precision=lax.Precision.HIGHEST)
    logits = weighted * final_scale
    live = (position[None, :] < row_lengths[:, None]).reshape(tokens.shape[0], 1)
    objective_scores = jnp.where(live, logits, jnp.float32(0.0))
    return (resid_out, objective_scores)
```

```python
import jax
import jax.numpy as jnp
from jax import lax
from jax.experimental import pallas as pl
from jax.experimental.pallas import tpu as pltpu
from jax.sharding import Mesh
from jax.sharding import PartitionSpec as P

HEAD = 128
EPS = 1e-05
WIDTH = 8192
NZ, NYH, NYL, NX, NC = 8, 4, 2, 4, 2
TP = ("z", "yh")
REP = ("yl", "x", "c")
VMEM = 48 * 1024 * 1024
F32 = jnp.float32
BF16 = jnp.bfloat16


def copies(x, axis, count):
    return lax.all_to_all(jnp.broadcast_to(x[None], (count, *x.shape)), axis, 0, 0)


def head_perm(k):
    pairs = []
    for yh in range(NYH):
        for c in range(NC):
            b = (yh // 2 + k) % 2
            pairs.append((yh * NC + c, (2 * c + b) * NC + yh % 2))
    return pairs


def kv_perm(k):
    pairs = []
    for z in range(NZ):
        for yh in range(NYH):
            for c in range(NC):
                zn, yn = (z % 2) * 4 + yh, z // 2
                b = (yn // 2 + k) % 2
                dest = (zn * NYH + 2 * c + b) * NC + yn % 2
                pairs.append(((z * NYH + yh) * NC + c, dest))
    return pairs


def split_sum(total):
    high = total.astype(BF16)
    low = (total - high.astype(F32)).astype(BF16)
    return high, low


def project_kernel(core_ref, x_ref, own_ref, other_ref, q_ref, kv_ref, qacc, kvacc):
    step = pl.program_id(0)

    @pl.when(step == 0)
    def _():
        qacc[...] = jnp.zeros_like(qacc)
        kvacc[...] = jnp.zeros_like(kvacc)

    x = x_ref[0]
    for side, w_ref in enumerate((own_ref, other_ref)):
        q = jnp.concatenate(
            [
                jnp.concatenate([w_ref[0, 0:128, 0:128], w_ref[0, 0:128, 128:256]], axis=0),
                jnp.concatenate([w_ref[0, 128:256, 0:128], w_ref[0, 128:256, 128:256]], axis=0),
            ],
            axis=1,
        )
        qacc[side] += jnp.dot(x, q, preferred_element_type=F32)
        kvacc[side] += lax.dot_general(
            w_ref[0, 256:320, :], x, (((1,), (1,)), ((), ())), preferred_element_type=F32
        )

    @pl.when(step == NZ - 1)
    def _():
        core = core_ref[0]
        for side in range(2):
            d = core if side == 0 else 1 - core
            for hi in range(2):
                q_ref[2 * hi + d] = qacc[side, :, hi * 128 : (hi + 1) * 128].astype(BF16)
                kv_ref[2 * hi + d] = kvacc[side, hi * 32 : (hi + 1) * 32, :].astype(BF16)


def project(core, x, own, other):
    rows = x.shape[1]
    return pl.pallas_call(
        project_kernel,
        grid=(NZ,),
        in_specs=[
            pl.BlockSpec(memory_space=pltpu.SMEM),
            pl.BlockSpec((1, rows, 256), lambda i: (i, 0, 0)),
            pl.BlockSpec((1, 320, 256), lambda i: (i, 0, 0)),
            pl.BlockSpec((1, 320, 256), lambda i: (i, 0, 0)),
        ],
        out_specs=[
            pl.BlockSpec((4, rows, 128), lambda i: (0, 0, 0)),
            pl.BlockSpec((4, 32, rows), lambda i: (0, 0, 0)),
        ],
        out_shape=[
            jax.ShapeDtypeStruct((4, rows, 128), BF16),
            jax.ShapeDtypeStruct((4, 32, rows), BF16),
        ],
        scratch_shapes=[pltpu.VMEM((2, rows, 256), F32), pltpu.VMEM((2, 64, rows), F32)],
        compiler_params=pltpu.CompilerParams(vmem_limit_bytes=VMEM),
        cost_estimate=pl.CostEstimate(flops=2 * rows * 2048 * 640, bytes_accessed=5_000_000, transcendentals=0),
    )(core, x, own, other)


def attention_kernel(len_ref, q_ref, kv_ref, out_ref):
    rows = q_ref.shape[1]
    half = rows // 2
    kv = kv_ref[...]
    stats = jnp.sum(kv[:, 32:48, :].astype(F32), axis=0)
    scale = lax.rsqrt((stats[0:1] + stats[1:2]) * (1.0 / WIDTH) + EPS)
    wide = jnp.broadcast_to(scale, (HEAD, rows))
    key = (kv[:, 0:16, :].reshape(HEAD, rows).astype(F32) * wide).astype(BF16)
    value = (kv[:, 16:32, :].reshape(HEAD, rows).astype(F32) * wide).astype(BF16)
    q = jnp.sum(q_ref[...].astype(F32), axis=0)
    q = (q * wide.T).astype(BF16)
    scores = jnp.dot(q, key, preferred_element_type=F32) * (1.0 / HEAD**0.5)
    i = lax.broadcasted_iota(jnp.int32, (rows, rows), 0)
    j = lax.broadcasted_iota(jnp.int32, (rows, rows), 1)
    limit = jnp.where(j < half, len_ref[0], half + len_ref[1])
    allowed = (j <= i) & (j < limit) & ((i < half) | (j >= half))
    scores = jnp.where(allowed, scores, F32(-1e30))
    scores = scores - jnp.max(scores, axis=1, keepdims=True)
    expo = jnp.exp(scores)
    probs = (expo / jnp.sum(expo, axis=1, keepdims=True)).astype(BF16)
    out = lax.dot_general(probs, value, (((1,), (1,)), ((), ())), preferred_element_type=F32)
    out_ref[...] = out.astype(BF16)


def attention(lengths, q, kv):
    rows = q.shape[1]
    return pl.pallas_call(
        attention_kernel,
        in_specs=[
            pl.BlockSpec(memory_space=pltpu.SMEM),
            pl.BlockSpec(memory_space=pltpu.VMEM),
            pl.BlockSpec(memory_space=pltpu.VMEM),
        ],
        out_specs=pl.BlockSpec(memory_space=pltpu.VMEM),
        out_shape=jax.ShapeDtypeStruct((rows, HEAD), BF16),
        compiler_params=pltpu.CompilerParams(vmem_limit_bytes=VMEM),
        cost_estimate=pl.CostEstimate(flops=4 * rows * rows * 128, bytes_accessed=800_000, transcendentals=rows * rows),
    )(lengths, q, kv)


def output_kernel(core_ref, a_ref, own_ref, other_ref, out_ref, acc):
    step = pl.program_id(0)

    @pl.when(step == 0)
    def _():
        acc[...] = jnp.zeros_like(acc)

    a = jnp.concatenate([a_ref[0], a_ref[1]], axis=1)
    for side, w_ref in enumerate((own_ref, other_ref)):
        for hi in range(2):
            w = jnp.concatenate(
                [w_ref[0, hi * 128 : (hi + 1) * 128], w_ref[1, hi * 128 : (hi + 1) * 128]], axis=0
            )
            acc[side, hi] += jnp.dot(a, w, preferred_element_type=F32)

    @pl.when(step == NZ // 2 - 1)
    def _():
        core = core_ref[0]
        for side in range(2):
            d = core if side == 0 else 1 - core
            for hi in range(2):
                out_ref[2 * hi + d] = acc[side, hi].astype(BF16)


def output_products(core, attended, own, other):
    rows = attended.shape[1]
    return pl.pallas_call(
        output_kernel,
        grid=(NZ // 2,),
        in_specs=[
            pl.BlockSpec(memory_space=pltpu.SMEM),
            pl.BlockSpec((2, rows, 128), lambda i: (i, 0, 0)),
            pl.BlockSpec((2, 256, 256), lambda i: (i, 0, 0)),
            pl.BlockSpec((2, 256, 256), lambda i: (i, 0, 0)),
        ],
        out_specs=pl.BlockSpec((4, rows, 256), lambda i: (0, 0, 0)),
        out_shape=jax.ShapeDtypeStruct((4, rows, 256), BF16),
        scratch_shapes=[pltpu.VMEM((2, 2, rows, 256), F32)],
        compiler_params=pltpu.CompilerParams(vmem_limit_bytes=VMEM),
        cost_estimate=pl.CostEstimate(flops=2 * rows * 1024 * 1024, bytes_accessed=4_000_000, transcendentals=0),
    )(core, attended, own, other)


def resid_kernel(p_ref, x_ref, head_ref, resid_ref, stat_ref):
    update = jnp.sum(p_ref[...].astype(F32), axis=0)
    resid = (x_ref[...].astype(F32) + update).astype(BF16)
    resid_ref[...] = resid
    r = resid.astype(F32)
    nt = (((1,), (1,)), ((), ()))
    scores = lax.dot_general(
        head_ref[...], r, nt, precision=lax.Precision.HIGHEST, preferred_element_type=F32
    )
    ones = jnp.ones((8, r.shape[1]), F32)
    squares = lax.dot_general(
        ones, r * r, nt, precision=lax.Precision.HIGHEST, preferred_element_type=F32
    )
    row = lax.broadcasted_iota(jnp.int32, scores.shape, 0)
    stat_ref[...] = jnp.where(row < 6, scores, squares)


def resid_and_stats(parts, tokens, heads):
    rows, cols = tokens.shape
    return pl.pallas_call(
        resid_kernel,
        in_specs=[pl.BlockSpec(memory_space=pltpu.VMEM)] * 3,
        out_specs=[pl.BlockSpec(memory_space=pltpu.VMEM)] * 2,
        out_shape=[
            jax.ShapeDtypeStruct((rows, cols), BF16),
            jax.ShapeDtypeStruct((8, rows), F32),
        ],
        compiler_params=pltpu.CompilerParams(vmem_limit_bytes=VMEM),
        cost_estimate=pl.CostEstimate(flops=2 * rows * cols * 96, bytes_accessed=1_200_000, transcendentals=0),
    )(parts, tokens, heads)


def local(
    tokens,
    row_lengths,
    attn_gain,
    query_weight,
    key_weight,
    value_matrix,
    output_weight,
    final_gain,
    value_head,
):
    rows = tokens.shape[0]
    z, yh, c = lax.axis_index("z"), lax.axis_index("yh"), lax.axis_index("c")
    core = c.astype(jnp.int32)[None]

    xf = tokens.astype(F32)
    gained = (xf * attn_gain[None, :]).astype(BF16)
    squares = jnp.sum(xf * xf, axis=1)

    with jax.named_scope("weights_out"):
        blocks = []
        for b in range(2):
            q = query_weight[256 * b : 256 * (b + 1)]
            q = jnp.concatenate([q[:128], q[128:]], axis=1)
            blocks.append(jnp.concatenate([q, output_weight[128 * b : 128 * (b + 1)]], axis=0))
        kv_t = jnp.concatenate([key_weight.T, value_matrix.T], axis=0)
        kv_blocks = [kv_t[:, :256], kv_t[:, 256:]]
        first = (yh // 2) == 0
        kv_first = (z // 4) == 0
        came = [
            lax.ppermute(
                jnp.where(first, blocks[k], blocks[1 - k]), ("yh", "c"), head_perm(k)
            )
            for k in range(2)
        ]
        kv_came = [
            lax.ppermute(
                jnp.where(kv_first, kv_blocks[k], kv_blocks[1 - k]), ("z", "yh", "c"), kv_perm(k)
            )
            for k in range(2)
        ]
        even = (yh % 2) == 0
        w = [jnp.where(even, came[k], came[1 - k]) for k in range(2)]
        kvw = [jnp.where(even, kv_came[k], kv_came[1 - k]) for k in range(2)]
        qkv_part = jnp.concatenate([w[0][:128], w[1][:128], kvw[0], kvw[1]], axis=0)
        out_part = jnp.concatenate([w[0][128:], w[1][128:]], axis=0)

    swap = [(0, 1), (1, 0)]
    with jax.named_scope("tokens_z"):
        x_all = copies(gained, "z", NZ)
    with jax.named_scope("qkv_rep"):
        qkv_own = copies(qkv_part, ("yl", "x"), NYL * NX)
        qkv_other = lax.ppermute(qkv_own, "c", swap)
    with jax.named_scope("out_rep"):
        out_own = copies(out_part, ("yl", "x"), NYL * NX)
        out_other = lax.ppermute(out_own, "c", swap)

    q_parts, kv_parts = project(core, x_all, qkv_own, qkv_other)

    with jax.named_scope("kv_sum"):
        high, low = split_sum(squares)
        stat = jnp.concatenate([high[None], low[None], jnp.zeros((14, rows), BF16)], axis=0)
        kv_send = jnp.concatenate([kv_parts, jnp.broadcast_to(stat[None], (NYH, 16, rows))], axis=1)
        kv_sum = lax.all_to_all(kv_send, "yh", 0, 0).astype(F32).sum(axis=0)
        high, low = split_sum(kv_sum[32] + kv_sum[33])
        stat = jnp.concatenate([high[None], low[None], jnp.zeros((14, rows), BF16)], axis=0)
        kv_mine = jnp.concatenate([kv_sum[:32].astype(BF16), stat], axis=0)
    with jax.named_scope("kv_z"):
        kv_all = copies(kv_mine, "z", NZ)
    with jax.named_scope("q_sum"):
        q_all = lax.all_to_all(q_parts, "yh", 0, 0)

    attended = attention(row_lengths, q_all, kv_all)

    with jax.named_scope("attended_z"):
        attended_all = copies(attended, "z", NZ)
    parts = output_products(core, attended_all, out_own, out_other)
    with jax.named_scope("out_sum"):
        parts = lax.all_to_all(parts, "yh", 0, 0)

    heads = jnp.concatenate([(final_gain[:, None] * value_head).T, jnp.zeros((2, tokens.shape[1]), F32)], axis=0)
    resid_out, stat = resid_and_stats(parts, tokens, heads)

    with jax.named_scope("stat_yh"):
        stat = copies(stat, "yh", NYH).sum(axis=0)
    with jax.named_scope("stat_z"):
        stat = copies(stat, "z", NZ).sum(axis=0)
    logits = stat[:6] * lax.rsqrt(stat[6] / WIDTH + EPS)[None, :]
    position = jnp.arange(rows // row_lengths.shape[0], dtype=jnp.int32)
    live = (position[None, :] < row_lengths[:, None]).reshape(1, rows)
    scores = jnp.where(live, logits, F32(0.0)).T
    return resid_out, scores


def solution(mesh):
    split = Mesh(mesh.devices.reshape(NZ, NYH, NYL, NX, NC), TP + REP)
    in_specs = (
        P(REP, TP),
        P(REP),
        P(TP),
        P(REP, TP),
        P(REP, TP),
        P(REP, TP),
        P(REP, TP),
        P(TP),
        P(TP, None),
    )
    out_specs = (P(REP, TP), P(REP, None))
    return jax.shard_map(local, mesh=split, in_specs=in_specs, out_specs=out_specs, check_vma=False)
```

```python
import jax
import jax.numpy as jnp
from jax import lax
from jax.experimental import pallas as pl
from jax.experimental.pallas import tpu as pltpu
from jax.sharding import Mesh
from jax.sharding import PartitionSpec as P

HEAD = 128
EPS = 1e-05
WIDTH = 8192
NZ, NYH, NYL, NX, NC = 8, 4, 2, 4, 2
TP = ("z", "yh")
REP = ("yl", "x", "c")
VMEM = 48 * 1024 * 1024
F32 = jnp.float32
BF16 = jnp.bfloat16
NT = (((1,), (1,)), ((), ()))
OWN_COST = 30_000_000_000


def copies(x, axis, count):
    return lax.all_to_all(jnp.broadcast_to(x[None], (count, *x.shape)), axis, 0, 0)


def head_perm(k):
    pairs = []
    for yh in range(NYH):
        for c in range(NC):
            b = (yh // 2 + k) % 2
            pairs.append((yh * NC + c, (2 * c + b) * NC + yh % 2))
    return pairs


def kv_perm(k):
    pairs = []
    for z in range(NZ):
        for yh in range(NYH):
            for c in range(NC):
                zn, yn = (z % 2) * 4 + yh, z // 2
                b = (yn // 2 + k) % 2
                dest = (zn * NYH + 2 * c + b) * NC + yn % 2
                pairs.append(((z * NYH + yh) * NC + c, dest))
    return pairs


def split_sum(total):
    high = total.astype(BF16)
    low = (total - high.astype(F32)).astype(BF16)
    return high, low


def columns(w_ref, hi):
    return jnp.concatenate(
        [
            w_ref[k, hi * 128 : (hi + 1) * 128, half * 128 : (half + 1) * 128]
            for k in range(NZ)
            for half in range(2)
        ],
        axis=0,
    )


def project_side(x_ref, w_ref, sq_ref, out_ref, d):
    rows = x_ref.shape[1]
    x = jnp.concatenate([x_ref[k] for k in range(NZ)], axis=1)
    high, low = split_sum(sq_ref[...])
    stat = jnp.concatenate([high, low, jnp.zeros((14, rows), BF16)], axis=0)
    w = jnp.concatenate([columns(w_ref, hi) for hi in range(2)], axis=1)
    q = jnp.dot(x, w, preferred_element_type=F32).astype(BF16)
    kvw = jnp.concatenate([w_ref[k, 256:320, :] for k in range(NZ)], axis=1)
    kv = lax.dot_general(kvw, x, NT, preferred_element_type=F32).astype(BF16)
    for hi in range(2):
        out_ref[2 * hi + d, 0:rows, :] = q[:, hi * 128 : (hi + 1) * 128]
        one = jnp.concatenate([kv[hi * 32 : (hi + 1) * 32, :], stat], axis=0)
        for p in range(3):
            at = rows + 48 * p
            out_ref[2 * hi + d, at : at + 48, :] = one[:, 128 * p : 128 * (p + 1)]


def own_kernel(core_ref, x_ref, w_ref, sq_ref, out_ref):
    project_side(x_ref, w_ref, sq_ref, out_ref, core_ref[0])


def other_kernel(core_ref, x_ref, w_ref, sq_ref, first_ref, out_ref):
    core = core_ref[0]
    for hi in range(2):
        out_ref[2 * hi + core] = first_ref[2 * hi + core]
    project_side(x_ref, w_ref, sq_ref, out_ref, 1 - core)


def project(core, x, own, other, squares):
    rows = x.shape[1]
    vmem = pl.BlockSpec(memory_space=pltpu.VMEM)
    smem = pl.BlockSpec(memory_space=pltpu.SMEM)

    def call(kernel, flops, *args):
        return pl.pallas_call(
            kernel,
            in_specs=[smem] + [vmem] * (len(args) - 1),
            out_specs=vmem,
            out_shape=jax.ShapeDtypeStruct((4, rows + 144, 128), BF16),
            compiler_params=pltpu.CompilerParams(vmem_limit_bytes=VMEM),
            cost_estimate=pl.CostEstimate(flops=flops, bytes_accessed=3_000_000, transcendentals=0),
        )(*args)

    first = call(own_kernel, OWN_COST, core, x, own, squares)
    return call(other_kernel, 2 * rows * 2048 * 320, core, x, other, squares, first)


def sum_kernel(p_ref, out_ref):
    rows = p_ref.shape[1] - 144
    total = jnp.sum(p_ref[...].astype(F32), axis=0)
    parts = [total[0:rows].astype(BF16)]
    for p in range(3):
        part = total[rows + 48 * p : rows + 48 * (p + 1)]
        high, low = split_sum(part[32:33] + part[33:34])
        parts += [part[0:32].astype(BF16), high, low, jnp.zeros((14, 128), BF16)]
    whole = jnp.concatenate(parts, axis=0)
    for k in range(NZ):
        out_ref[k] = whole


def summed_copies(parts):
    return pl.pallas_call(
        sum_kernel,
        in_specs=[pl.BlockSpec(memory_space=pltpu.VMEM)],
        out_specs=pl.BlockSpec(memory_space=pltpu.VMEM),
        out_shape=jax.ShapeDtypeStruct((NZ, *parts.shape[1:]), BF16),
        compiler_params=pltpu.CompilerParams(vmem_limit_bytes=VMEM),
    )(parts)


def attend_kernel(core_ref, len_ref, m_ref, own_ref, other_ref, out_ref, att):
    rows = m_ref.shape[1] - 144
    half = rows // 2
    at = [rows + 48 * p for p in range(3)]
    stats = jnp.concatenate(
        [jnp.sum(m_ref[:, a + 32 : a + 48, :].astype(F32), axis=0) for a in at], axis=1
    )
    scale = lax.rsqrt((stats[0:1] + stats[1:2]) * (1.0 / WIDTH) + EPS)
    wide = jnp.broadcast_to(scale, (HEAD, rows))
    key = jnp.concatenate([m_ref[:, a : a + 16, :].reshape(HEAD, 128) for a in at], axis=1)
    key = (key.astype(F32) * wide).astype(BF16)
    value = jnp.concatenate([m_ref[:, a + 16 : a + 32, :].reshape(HEAD, 128) for a in at], axis=1)
    value = (value.astype(F32) * wide).astype(BF16)
    column = wide.T[:, 0:1] * (1.0 / HEAD**0.5)
    for seq in range(2):
        first = seq * 128
        k = key[:, first : first + 256]
        v = value[:, first : first + 256]
        i = lax.broadcasted_iota(jnp.int32, (half, 256), 0)
        j = lax.broadcasted_iota(jnp.int32, (half, 256), 1) - (seq * half - first)
        allowed = (j >= 0) & (j <= i) & (j < len_ref[seq])
        c = column[seq * half : (seq + 1) * half]
        for head in range(NZ):
            q = m_ref[head, seq * half : (seq + 1) * half, :]
            scores = jnp.dot(q, k, preferred_element_type=F32) * c
            scores = jnp.where(allowed, scores, F32(-1e30))
            scores = scores - jnp.max(scores, axis=1, keepdims=True)
            expo = jnp.exp(scores)
            probs = (expo * (1.0 / jnp.sum(expo, axis=1, keepdims=True))).astype(BF16)
            o = lax.dot_general(probs, v, NT, preferred_element_type=F32)
            att[seq * half : (seq + 1) * half, head * 128 : (head + 1) * 128] = o.astype(BF16)
    core = core_ref[0]
    a = att[...]
    for side, w_ref in enumerate((own_ref, other_ref)):
        d = core if side == 0 else 1 - core
        for hi in range(2):
            w = jnp.concatenate([w_ref[k, hi * 128 : (hi + 1) * 128] for k in range(NZ)], axis=0)
            out_ref[2 * hi + d] = jnp.dot(a, w, preferred_element_type=F32).astype(BF16)


def attend(core, lengths, messages, own, other):
    rows = messages.shape[1] - 144
    vmem = pl.BlockSpec(memory_space=pltpu.VMEM)
    smem = pl.BlockSpec(memory_space=pltpu.SMEM)
    return pl.pallas_call(
        attend_kernel,
        in_specs=[smem, smem, vmem, vmem, vmem],
        out_specs=vmem,
        out_shape=jax.ShapeDtypeStruct((4, rows, 256), BF16),
        scratch_shapes=[pltpu.VMEM((rows, NZ * HEAD), BF16)],
        compiler_params=pltpu.CompilerParams(vmem_limit_bytes=VMEM),
        cost_estimate=pl.CostEstimate(flops=2 * rows * 1024 * 1300, bytes_accessed=4_000_000, transcendentals=1_000_000),
    )(core, lengths, messages, own, other)


def resid_kernel(p_ref, x_ref, head_ref, resid_ref, stat_ref):
    update = jnp.sum(p_ref[...].astype(F32), axis=0)
    resid = (x_ref[...].astype(F32) + update).astype(BF16)
    resid_ref[...] = resid
    r = resid.astype(F32)
    scores = lax.dot_general(
        head_ref[...], r, NT, precision=lax.Precision.HIGHEST, preferred_element_type=F32
    )
    ones = jnp.ones((8, r.shape[1]), F32)
    squares = lax.dot_general(
        ones, r * r, NT, precision=lax.Precision.HIGHEST, preferred_element_type=F32
    )
    row = lax.broadcasted_iota(jnp.int32, scores.shape, 0)
    stat = jnp.where(row < 6, scores, squares).astype(BF16)
    for k in range(NZ * NYH):
        stat_ref[k] = stat


def resid_and_stats(parts, tokens, heads):
    rows, cols = tokens.shape
    return pl.pallas_call(
        resid_kernel,
        in_specs=[pl.BlockSpec(memory_space=pltpu.VMEM)] * 3,
        out_specs=[pl.BlockSpec(memory_space=pltpu.VMEM)] * 2,
        out_shape=[
            jax.ShapeDtypeStruct((rows, cols), BF16),
            jax.ShapeDtypeStruct((NZ * NYH, 8, rows), BF16),
        ],
        compiler_params=pltpu.CompilerParams(vmem_limit_bytes=VMEM),
        cost_estimate=pl.CostEstimate(flops=2 * rows * cols * 96, bytes_accessed=1_200_000, transcendentals=0),
    )(parts, tokens, heads)


def local(
    tokens,
    row_lengths,
    attn_gain,
    query_weight,
    key_weight,
    value_matrix,
    output_weight,
    final_gain,
    value_head,
):
    rows = tokens.shape[0]
    z, yh, c = lax.axis_index("z"), lax.axis_index("yh"), lax.axis_index("c")
    core = c.astype(jnp.int32)[None]

    xf = tokens.astype(F32)
    gained = (xf * attn_gain[None, :]).astype(BF16)
    squares = jnp.sum(xf * xf, axis=1)[None, :]

    with jax.named_scope("weights_out"):
        blocks = []
        for b in range(2):
            q = query_weight[256 * b : 256 * (b + 1)]
            q = jnp.concatenate([q[:128], q[128:]], axis=1)
            blocks.append(jnp.concatenate([q, output_weight[128 * b : 128 * (b + 1)]], axis=0))
        kv_t = jnp.concatenate([key_weight.T, value_matrix.T], axis=0)
        kv_blocks = [kv_t[:, :256], kv_t[:, 256:]]
        first = (yh // 2) == 0
        kv_first = (z // 4) == 0
        came = [
            lax.ppermute(
                jnp.where(first, blocks[k], blocks[1 - k]), ("yh", "c"), head_perm(k)
            )
            for k in range(2)
        ]
        kv_came = [
            lax.ppermute(
                jnp.where(kv_first, kv_blocks[k], kv_blocks[1 - k]), ("z", "yh", "c"), kv_perm(k)
            )
            for k in range(2)
        ]
        even = (yh % 2) == 0
        w = [jnp.where(even, came[k], came[1 - k]) for k in range(2)]
        kvw = [jnp.where(even, kv_came[k], kv_came[1 - k]) for k in range(2)]
        qkv_part = jnp.concatenate([w[0][:128], w[1][:128], kvw[0], kvw[1]], axis=0)
        out_part = jnp.concatenate([w[0][128:], w[1][128:]], axis=0)

    swap = [(0, 1), (1, 0)]
    with jax.named_scope("tokens_z"):
        x_all = lax.all_gather(gained, "z", axis=0)
    with jax.named_scope("qkv_rep"):
        qkv_own = copies(qkv_part, ("yl", "x"), NYL * NX)
        qkv_other = lax.ppermute(qkv_own, "c", swap)
    with jax.named_scope("out_rep"):
        out_own = lax.all_gather(out_part, ("yl", "x"), axis=0)
        out_other = lax.ppermute(out_own, "c", swap)

    parts = project(core, x_all, qkv_own, qkv_other, squares)
    with jax.named_scope("qkv_sum"):
        parts = lax.all_to_all(parts, "yh", 0, 0)
    with jax.named_scope("qkv_z"):
        messages = lax.all_to_all(summed_copies(parts), "z", 0, 0)
    parts = attend(core, row_lengths, messages, out_own, out_other)
    with jax.named_scope("out_sum"):
        parts = lax.all_to_all(parts, "yh", 0, 0)

    heads = jnp.concatenate([(final_gain[:, None] * value_head).T, jnp.zeros((2, tokens.shape[1]), F32)], axis=0)
    resid_out, stat = resid_and_stats(parts, tokens, heads)

    with jax.named_scope("stat_tp"):
        stat = lax.all_to_all(stat, TP, 0, 0).astype(F32).sum(axis=0)
    logits = stat[:6] * lax.rsqrt(stat[6] / WIDTH + EPS)[None, :]
    position = jnp.arange(rows // row_lengths.shape[0], dtype=jnp.int32)
    live = (position[None, :] < row_lengths[:, None]).reshape(1, rows)
    scores = jnp.where(live, logits, F32(0.0)).T
    return resid_out, scores


def solution(mesh):
    split = Mesh(mesh.devices.reshape(NZ, NYH, NYL, NX, NC), TP + REP)
    in_specs = (
        P(REP, TP),
        P(REP),
        P(TP),
        P(REP, TP),
        P(REP, TP),
        P(REP, TP),
        P(REP, TP),
        P(TP),
        P(TP, None),
    )
    out_specs = (P(REP, TP), P(REP, None))
    return jax.shard_map(local, mesh=split, in_specs=in_specs, out_specs=out_specs, check_vma=False)
```

```python
import jax
import jax.numpy as jnp
from jax import lax
from jax.experimental import pallas as pl
from jax.experimental.pallas import tpu as pltpu
from jax.sharding import Mesh
from jax.sharding import PartitionSpec as P

HEAD = 128
EPS = 1e-05
WIDTH = 8192
NZ, NYH, NYL, NX, NC = 8, 4, 2, 4, 2
TP = ("z", "yh")
REP = ("yl", "x", "c")
VMEM = 48 * 1024 * 1024
F32 = jnp.float32
BF16 = jnp.bfloat16
NT = (((1,), (1,)), ((), ()))
OWN_COST = 30_000_000_000
ATTEND_COST = 8_000_000_000


def copies(x, axis, count):
    return lax.all_to_all(jnp.broadcast_to(x[None], (count, *x.shape)), axis, 0, 0)


def head_perm(k):
    pairs = []
    for yh in range(NYH):
        for c in range(NC):
            b = (yh // 2 + k) % 2
            pairs.append((yh * NC + c, (2 * c + b) * NC + yh % 2))
    return pairs


def kv_perm():
    return [
        (z * NYH + yh, ((z % 2) * 4 + yh) * NYH + z // 2) for z in range(NZ) for yh in range(NYH)
    ]


def split_sum(total):
    high = total.astype(BF16)
    low = (total - high.astype(F32)).astype(BF16)
    return high, low


def pack_kernel(odd_ref, q0, q1, out_ref):
    even = odd_ref[0] == 0
    first, second = jnp.where(even, q0[...], q1[...]), jnp.where(even, q1[...], q0[...])
    whole = jnp.concatenate([first[:128], second[:128], first[128:], second[128:]], axis=0)
    for k in range(NYL * NX):
        out_ref[k] = whole


def packed_copies(odd, *parts):
    vmem = pl.BlockSpec(memory_space=pltpu.VMEM)
    return pl.pallas_call(
        pack_kernel,
        in_specs=[pl.BlockSpec(memory_space=pltpu.SMEM)] + [vmem] * 2,
        out_specs=vmem,
        out_shape=jax.ShapeDtypeStruct((NYL * NX, 320, 256), BF16),
        compiler_params=pltpu.CompilerParams(vmem_limit_bytes=VMEM),
        cost_estimate=pl.CostEstimate(flops=1000, bytes_accessed=1000, transcendentals=0),
    )(odd, *parts)


def columns(w_ref, hi):
    return jnp.concatenate(
        [
            w_ref[k, hi * 128 : (hi + 1) * 128, half * 128 : (half + 1) * 128]
            for k in range(NZ)
            for half in range(2)
        ],
        axis=0,
    )


def project_side(x_ref, w_ref, stat, out_ref, d):
    rows = x_ref.shape[1]
    x = jnp.concatenate([x_ref[k] for k in range(NZ)], axis=1)
    w = jnp.concatenate([columns(w_ref, hi) for hi in range(2)], axis=1)
    q = jnp.dot(x, w, preferred_element_type=F32).astype(BF16)
    kvw = jnp.concatenate([w_ref[k, 256:320, :] for k in range(NZ)], axis=1)
    kv = lax.dot_general(kvw, x, NT, preferred_element_type=F32).astype(BF16)
    for hi in range(2):
        out_ref[2 * hi + d, 0:rows, :] = q[:, hi * 128 : (hi + 1) * 128]
        for p in range(3):
            at = rows + 32 * p
            out_ref[2 * hi + d, at : at + 32, :] = kv[hi * 32 : (hi + 1) * 32, 128 * p : 128 * (p + 1)]
        out_ref[2 * hi + d, rows + 96 : rows + 112, :] = stat


def stat_rows(sums):
    pairs = [half for one in sums for half in split_sum(one)]
    return jnp.concatenate(pairs + [jnp.zeros((10, 128), BF16)], axis=0)


def own_kernel(core_ref, x_ref, w_ref, tokens_ref, out_ref):
    t = tokens_ref[...].astype(F32)
    ones = jnp.ones((8, t.shape[1]), F32)
    sq = lax.dot_general(
        ones, t * t, NT, precision=lax.Precision.HIGHEST, preferred_element_type=F32
    )
    stat = stat_rows([sq[0:1, 128 * p : 128 * (p + 1)] for p in range(3)])
    project_side(x_ref, w_ref, stat, out_ref, core_ref[0])


def other_kernel(core_ref, x_ref, w_ref, first_ref, out_ref):
    core = core_ref[0]
    rows = x_ref.shape[1]
    for hi in range(2):
        out_ref[2 * hi + core] = first_ref[2 * hi + core]
    project_side(x_ref, w_ref, first_ref[core, rows + 96 : rows + 112, :], out_ref, 1 - core)


def project(core, x, own, other, tokens):
    rows = x.shape[1]
    vmem = pl.BlockSpec(memory_space=pltpu.VMEM)
    smem = pl.BlockSpec(memory_space=pltpu.SMEM)

    def call(kernel, flops, *args):
        return pl.pallas_call(
            kernel,
            in_specs=[smem] + [vmem] * (len(args) - 1),
            out_specs=vmem,
            out_shape=jax.ShapeDtypeStruct((4, rows + 112, 128), BF16),
            compiler_params=pltpu.CompilerParams(vmem_limit_bytes=VMEM),
            cost_estimate=pl.CostEstimate(flops=flops, bytes_accessed=3_000_000, transcendentals=0),
        )(*args)

    first = call(own_kernel, OWN_COST, core, x, own, tokens)
    return call(other_kernel, 2 * rows * 2048 * 320, core, x, other, first)


def sum_kernel(p_ref, out_ref):
    rows = p_ref.shape[1] - 112
    total = jnp.sum(p_ref[...].astype(F32), axis=0)
    out_ref[0 : rows + 96, :] = total[0 : rows + 96].astype(BF16)
    at = rows + 96
    sums = [total[at + 2 * p : at + 2 * p + 1] + total[at + 2 * p + 1 : at + 2 * p + 2] for p in range(3)]
    out_ref[at : at + 16, :] = stat_rows(sums)


def summed(parts):
    return pl.pallas_call(
        sum_kernel,
        in_specs=[pl.BlockSpec(memory_space=pltpu.VMEM)],
        out_specs=pl.BlockSpec(memory_space=pltpu.VMEM),
        out_shape=jax.ShapeDtypeStruct(parts.shape[1:], BF16),
        compiler_params=pltpu.CompilerParams(vmem_limit_bytes=VMEM),
    )(parts)


def attend_kernel(len_ref, m_ref, att_ref):
    rows = m_ref.shape[1] - 112
    half = rows // 2
    at = [rows + 32 * p for p in range(3)]
    stats = jnp.sum(m_ref[:, rows + 96 : rows + 112, :].astype(F32), axis=0)
    stats = jnp.concatenate(
        [stats[2 * p : 2 * p + 1] + stats[2 * p + 1 : 2 * p + 2] for p in range(3)], axis=1
    )
    scale = lax.rsqrt(stats * (1.0 / WIDTH) + EPS)
    wide = jnp.broadcast_to(scale, (HEAD, rows))
    key = jnp.concatenate([m_ref[:, a : a + 16, :].reshape(HEAD, 128) for a in at], axis=1)
    key = (key.astype(F32) * wide).astype(BF16)
    value = jnp.concatenate([m_ref[:, a + 16 : a + 32, :].reshape(HEAD, 128) for a in at], axis=1)
    value = (value.astype(F32) * wide).astype(BF16)
    column = wide.T[:, 0:1] * (1.0 / HEAD**0.5)
    for seq in range(2):
        first = seq * 128
        k = key[:, first : first + 256]
        v = value[:, first : first + 256]
        i = lax.broadcasted_iota(jnp.int32, (half, 256), 0)
        j = lax.broadcasted_iota(jnp.int32, (half, 256), 1) - (seq * half - first)
        allowed = (j >= 0) & (j <= i) & (j < len_ref[seq])
        c = column[seq * half : (seq + 1) * half]
        for head in range(NZ):
            q = m_ref[head, seq * half : (seq + 1) * half, :]
            scores = jnp.dot(q, k, preferred_element_type=F32) * c
            scores = jnp.where(allowed, scores, F32(-1e30))
            scores = scores - jnp.max(scores, axis=1, keepdims=True)
            expo = jnp.exp(scores)
            probs = (expo * (1.0 / jnp.sum(expo, axis=1, keepdims=True))).astype(BF16)
            o = lax.dot_general(probs, v, NT, preferred_element_type=F32)
            att_ref[seq * half : (seq + 1) * half, head * 128 : (head + 1) * 128] = o.astype(BF16)


def output_side(a, w_ref, out_ref, d):
    for hi in range(2):
        w = jnp.concatenate([w_ref[k, hi * 128 : (hi + 1) * 128] for k in range(NZ)], axis=0)
        out_ref[2 * hi + d] = jnp.dot(a, w, preferred_element_type=F32).astype(BF16)


def output_kernel(core_ref, att_ref, own_ref, other_ref, out_ref):
    core = core_ref[0]
    output_side(att_ref[...], own_ref, out_ref, core)
    output_side(att_ref[...], other_ref, out_ref, 1 - core)


def attend(lengths, messages):
    rows = messages.shape[1] - 112
    vmem = pl.BlockSpec(memory_space=pltpu.VMEM)
    smem = pl.BlockSpec(memory_space=pltpu.SMEM)
    return pl.pallas_call(
        attend_kernel,
        in_specs=[smem, vmem],
        out_specs=vmem,
        out_shape=jax.ShapeDtypeStruct((rows, NZ * HEAD), BF16),
        compiler_params=pltpu.CompilerParams(vmem_limit_bytes=VMEM),
        cost_estimate=pl.CostEstimate(flops=ATTEND_COST, bytes_accessed=2_000_000, transcendentals=1_000_000),
    )(lengths, messages)


def output_products(core, attended, own, other):
    rows = attended.shape[0]
    vmem = pl.BlockSpec(memory_space=pltpu.VMEM)
    smem = pl.BlockSpec(memory_space=pltpu.SMEM)
    return pl.pallas_call(
        output_kernel,
        in_specs=[smem, vmem, vmem, vmem],
        out_specs=vmem,
        out_shape=jax.ShapeDtypeStruct((4, rows, 256), BF16),
        compiler_params=pltpu.CompilerParams(vmem_limit_bytes=VMEM),
        cost_estimate=pl.CostEstimate(flops=2 * rows * 1024 * 1024, bytes_accessed=5_000_000, transcendentals=0),
    )(core, attended, own, other)


def resid_kernel(p_ref, x_ref, head_ref, resid_ref, stat_ref):
    update = jnp.sum(p_ref[...].astype(F32), axis=0)
    resid = (x_ref[...].astype(F32) + update).astype(BF16)
    resid_ref[...] = resid
    r = resid.astype(F32)
    scores = lax.dot_general(
        head_ref[...], r, NT, precision=lax.Precision.HIGHEST, preferred_element_type=F32
    )
    ones = jnp.ones((8, r.shape[1]), F32)
    squares = lax.dot_general(
        ones, r * r, NT, precision=lax.Precision.HIGHEST, preferred_element_type=F32
    )
    row = lax.broadcasted_iota(jnp.int32, scores.shape, 0)
    stat = jnp.where(row < 6, scores, squares).astype(BF16)
    for k in range(NZ * NYH):
        stat_ref[k] = stat


def resid_and_stats(parts, tokens, heads):
    rows, cols = tokens.shape
    return pl.pallas_call(
        resid_kernel,
        in_specs=[pl.BlockSpec(memory_space=pltpu.VMEM)] * 3,
        out_specs=[pl.BlockSpec(memory_space=pltpu.VMEM)] * 2,
        out_shape=[
            jax.ShapeDtypeStruct((rows, cols), BF16),
            jax.ShapeDtypeStruct((NZ * NYH, 8, rows), BF16),
        ],
        compiler_params=pltpu.CompilerParams(vmem_limit_bytes=VMEM),
        cost_estimate=pl.CostEstimate(flops=2 * rows * cols * 96, bytes_accessed=1_200_000, transcendentals=0),
    )(parts, tokens, heads)


def local(
    tokens,
    row_lengths,
    attn_gain,
    query_weight,
    key_weight,
    value_matrix,
    output_weight,
    final_gain,
    value_head,
):
    rows = tokens.shape[0]
    z, yh, c = lax.axis_index("z"), lax.axis_index("yh"), lax.axis_index("c")
    core = c.astype(jnp.int32)[None]

    xf = tokens.astype(F32)
    gained = (xf * attn_gain[None, :]).astype(BF16)

    first, even = (yh // 2) == 0, (yh % 2) == 0
    with jax.named_scope("weights_yh"):
        kv = lax.ppermute(jnp.concatenate([key_weight.T, value_matrix.T], axis=0), TP, kv_perm())
        q = [query_weight[256 * b : 256 * (b + 1)] for b in range(2)]
        q = [
            jnp.concatenate(
                [q[b][:128], q[b][128:]], axis=1
            )
            for b in range(2)
        ]
        q = [jnp.concatenate([q[b], kv[:, 256 * b : 256 * (b + 1)]], axis=0) for b in range(2)]
        q = [
            lax.ppermute(jnp.where(first, q[k], q[1 - k]), ("yh", "c"), head_perm(k))
            for k in range(2)
        ]
        odd = (yh % 2).astype(jnp.int32)[None]
        qkv_send = packed_copies(odd, *q)
    with jax.named_scope("out_yh"):
        o = [output_weight[:128], output_weight[128:]]
        o = [jnp.where(first, o[k], o[1 - k]) for k in range(2)]
        o, qkv_send = lax.optimization_barrier((o, qkv_send))
        o = [lax.ppermute(o[k], ("yh", "c"), head_perm(k)) for k in range(2)]


    swap = [(0, 1), (1, 0)]
    with jax.named_scope("tokens_z"):
        x_all = lax.all_gather(gained, "z", axis=0)
    with jax.named_scope("qkv_rep"):
        qkv_own = lax.all_to_all(qkv_send, ("yl", "x"), 0, 0)
        qkv_other = lax.ppermute(qkv_own, "c", swap)
    with jax.named_scope("out_rep"):
        o, x_all = lax.optimization_barrier((o, x_all))
        out_part = jnp.concatenate([jnp.where(even, o[k], o[1 - k]) for k in range(2)], axis=0)
        out_own = lax.all_gather(out_part, ("yl", "x"), axis=0)
    parts = project(core, x_all, qkv_own, qkv_other, tokens)
    with jax.named_scope("qkv_sum"):
        parts = lax.all_to_all(parts, "yh", 0, 0)
    with jax.named_scope("qkv_z"):
        messages = lax.all_gather(summed(parts), "z", axis=0)
    out_own, messages = lax.optimization_barrier((out_own, messages))
    out_other = lax.ppermute(out_own, "c", swap)
    attended = attend(row_lengths, messages)
    parts = output_products(core, attended, out_own, out_other)
    with jax.named_scope("out_sum"):
        parts = lax.all_to_all(parts, "yh", 0, 0)

    heads = jnp.concatenate([(final_gain[:, None] * value_head).T, jnp.zeros((2, tokens.shape[1]), F32)], axis=0)
    resid_out, stat = resid_and_stats(parts, tokens, heads)

    with jax.named_scope("stat_tp"):
        stat = lax.all_to_all(stat, TP, 0, 0).astype(F32).sum(axis=0)
    logits = stat[:6] * lax.rsqrt(stat[6] / WIDTH + EPS)[None, :]
    position = jnp.arange(rows // row_lengths.shape[0], dtype=jnp.int32)
    live = (position[None, :] < row_lengths[:, None]).reshape(1, rows)
    scores = jnp.where(live, logits, F32(0.0)).T
    return resid_out, scores


def solution(mesh):
    split = Mesh(mesh.devices.reshape(NZ, NYH, NYL, NX, NC), TP + REP)
    in_specs = (
        P(REP, TP),
        P(REP),
        P(TP),
        P(REP, TP),
        P(REP, TP),
        P(REP, TP),
        P(REP, TP),
        P(TP),
        P(TP, None),
    )
    out_specs = (P(REP, TP), P(REP, None))
    return jax.shard_map(local, mesh=split, in_specs=in_specs, out_specs=out_specs, check_vma=False)
```

```python
import jax
import jax.numpy as jnp
from jax import lax
from jax.experimental import pallas as pl
from jax.experimental.pallas import tpu as pltpu
from jax.sharding import Mesh
from jax.sharding import PartitionSpec as P

HEAD = 128
EPS = 1e-05
WIDTH = 8192
NZ, NYH, NYL, NX, NC = 8, 4, 2, 4, 2
TP = ("z", "yh")
REP = ("yl", "x", "c")
VMEM = 48 * 1024 * 1024
F32 = jnp.float32
BF16 = jnp.bfloat16
NT = (((1,), (1,)), ((), ()))
OWN_COST = 30_000_000_000
ATTEND_COST = 8_000_000_000


def copies(x, axis, count):
    return lax.all_to_all(jnp.broadcast_to(x[None], (count, *x.shape)), axis, 0, 0)


def head_perm(k):
    pairs = []
    for yh in range(NYH):
        for c in range(NC):
            b = (yh // 2 + k) % 2
            pairs.append((yh * NC + c, (2 * c + b) * NC + yh % 2))
    return pairs


def kv_perm():
    return [
        (z * NYH + yh, ((z % 2) * 4 + yh) * NYH + z // 2) for z in range(NZ) for yh in range(NYH)
    ]


def split_sum(total):
    high = total.astype(BF16)
    low = (total - high.astype(F32)).astype(BF16)
    return high, low


def pack_kernel(odd_ref, q0, q1, out_ref):
    even = odd_ref[0] == 0
    first, second = jnp.where(even, q0[...], q1[...]), jnp.where(even, q1[...], q0[...])
    whole = jnp.concatenate([first[:128], second[:128], first[128:], second[128:]], axis=0)
    for k in range(NYL * NX):
        out_ref[k] = whole


def packed_copies(odd, *parts):
    vmem = pl.BlockSpec(memory_space=pltpu.VMEM)
    return pl.pallas_call(
        pack_kernel,
        in_specs=[pl.BlockSpec(memory_space=pltpu.SMEM)] + [vmem] * 2,
        out_specs=vmem,
        out_shape=jax.ShapeDtypeStruct((NYL * NX, 320, 256), BF16),
        compiler_params=pltpu.CompilerParams(vmem_limit_bytes=VMEM),
        cost_estimate=pl.CostEstimate(flops=1000, bytes_accessed=1000, transcendentals=0),
    )(odd, *parts)


def columns(w_ref, hi):
    return jnp.concatenate(
        [
            w_ref[k, hi * 128 : (hi + 1) * 128, half * 128 : (half + 1) * 128]
            for k in range(NZ)
            for half in range(2)
        ],
        axis=0,
    )


def project_side(x_ref, w_ref, stat, out_ref, d):
    rows = x_ref.shape[1]
    x = jnp.concatenate([x_ref[k] for k in range(NZ)], axis=1)
    w = jnp.concatenate([columns(w_ref, hi) for hi in range(2)], axis=1)
    q = jnp.dot(x, w, preferred_element_type=F32).astype(BF16)
    kvw = jnp.concatenate([w_ref[k, 256:320, :] for k in range(NZ)], axis=1)
    kv = lax.dot_general(kvw, x, NT, preferred_element_type=F32).astype(BF16)
    for hi in range(2):
        out_ref[2 * hi + d, 0:rows, :] = q[:, hi * 128 : (hi + 1) * 128]
        for p in range(3):
            at = rows + 32 * p
            out_ref[2 * hi + d, at : at + 32, :] = kv[hi * 32 : (hi + 1) * 32, 128 * p : 128 * (p + 1)]
        out_ref[2 * hi + d, rows + 96 : rows + 112, :] = stat


def stat_rows(sums):
    pairs = [half for one in sums for half in split_sum(one)]
    return jnp.concatenate(pairs + [jnp.zeros((10, 128), BF16)], axis=0)


def own_kernel(core_ref, x_ref, w_ref, tokens_ref, out_ref):
    t = tokens_ref[...].astype(F32)
    ones = jnp.ones((8, t.shape[1]), F32)
    sq = lax.dot_general(
        ones, t * t, NT, precision=lax.Precision.HIGHEST, preferred_element_type=F32
    )
    stat = stat_rows([sq[0:1, 128 * p : 128 * (p + 1)] for p in range(3)])
    project_side(x_ref, w_ref, stat, out_ref, core_ref[0])


def other_kernel(core_ref, x_ref, w_ref, first_ref, out_ref):
    core = core_ref[0]
    rows = x_ref.shape[1]
    for hi in range(2):
        out_ref[2 * hi + core] = first_ref[2 * hi + core]
    project_side(x_ref, w_ref, first_ref[core, rows + 96 : rows + 112, :], out_ref, 1 - core)


def project(core, x, own, other, tokens):
    rows = x.shape[1]
    vmem = pl.BlockSpec(memory_space=pltpu.VMEM)
    smem = pl.BlockSpec(memory_space=pltpu.SMEM)

    def call(kernel, flops, *args):
        return pl.pallas_call(
            kernel,
            in_specs=[smem] + [vmem] * (len(args) - 1),
            out_specs=vmem,
            out_shape=jax.ShapeDtypeStruct((4, rows + 112, 128), BF16),
            compiler_params=pltpu.CompilerParams(vmem_limit_bytes=VMEM),
            cost_estimate=pl.CostEstimate(flops=flops, bytes_accessed=3_000_000, transcendentals=0),
        )(*args)

    first = call(own_kernel, OWN_COST, core, x, own, tokens)
    return call(other_kernel, 2 * rows * 2048 * 320, core, x, other, first)


def sum_kernel(p_ref, out_ref):
    rows = p_ref.shape[1] - 112
    total = jnp.sum(p_ref[...].astype(F32), axis=0)
    out_ref[0 : rows + 96, :] = total[0 : rows + 96].astype(BF16)
    at = rows + 96
    sums = [total[at + 2 * p : at + 2 * p + 1] + total[at + 2 * p + 1 : at + 2 * p + 2] for p in range(3)]
    out_ref[at : at + 16, :] = stat_rows(sums)


def summed(parts):
    return pl.pallas_call(
        sum_kernel,
        in_specs=[pl.BlockSpec(memory_space=pltpu.VMEM)],
        out_specs=pl.BlockSpec(memory_space=pltpu.VMEM),
        out_shape=jax.ShapeDtypeStruct(parts.shape[1:], BF16),
        compiler_params=pltpu.CompilerParams(vmem_limit_bytes=VMEM),
    )(parts)


def attend_kernel(len_ref, m_ref, att_ref):
    rows = m_ref.shape[1] - 112
    half = rows // 2
    at = [rows + 32 * p for p in range(3)]
    stats = jnp.sum(m_ref[:, rows + 96 : rows + 112, :].astype(F32), axis=0)
    stats = jnp.concatenate(
        [stats[2 * p : 2 * p + 1] + stats[2 * p + 1 : 2 * p + 2] for p in range(3)], axis=1
    )
    scale = lax.rsqrt(stats * (1.0 / WIDTH) + EPS)
    wide = jnp.broadcast_to(scale, (HEAD, rows))
    key = jnp.concatenate([m_ref[:, a : a + 16, :].reshape(HEAD, 128) for a in at], axis=1)
    key = (key.astype(F32) * wide).astype(BF16)
    value = jnp.concatenate([m_ref[:, a + 16 : a + 32, :].reshape(HEAD, 128) for a in at], axis=1)
    value = (value.astype(F32) * wide).astype(BF16)
    column = wide.T[:, 0:1] * (1.0 / HEAD**0.5)
    for seq in range(2):
        first = seq * 128
        k = key[:, first : first + 256]
        v = value[:, first : first + 256]
        i = lax.broadcasted_iota(jnp.int32, (half, 256), 0)
        j = lax.broadcasted_iota(jnp.int32, (half, 256), 1) - (seq * half - first)
        allowed = (j >= 0) & (j <= i) & (j < len_ref[seq])
        c = column[seq * half : (seq + 1) * half]
        for head in range(NZ):
            q = m_ref[head, seq * half : (seq + 1) * half, :]
            scores = jnp.dot(q, k, preferred_element_type=F32) * c
            scores = jnp.where(allowed, scores, F32(-1e30))
            scores = scores - jnp.max(scores, axis=1, keepdims=True)
            expo = jnp.exp(scores)
            probs = (expo * (1.0 / jnp.sum(expo, axis=1, keepdims=True))).astype(BF16)
            o = lax.dot_general(probs, v, NT, preferred_element_type=F32)
            att_ref[seq * half : (seq + 1) * half, head * 128 : (head + 1) * 128] = o.astype(BF16)


def output_kernel(att_ref, w_ref, out_ref):
    a = att_ref[...]
    for d in range(2):
        for hi in range(2):
            w = jnp.concatenate(
                [w_ref[2 * k + d, hi * 128 : (hi + 1) * 128] for k in range(NZ)], axis=0
            )
            out_ref[2 * hi + d] = jnp.dot(a, w, preferred_element_type=F32).astype(BF16)


def attend(lengths, messages):
    rows = messages.shape[1] - 112
    vmem = pl.BlockSpec(memory_space=pltpu.VMEM)
    smem = pl.BlockSpec(memory_space=pltpu.SMEM)
    return pl.pallas_call(
        attend_kernel,
        in_specs=[smem, vmem],
        out_specs=vmem,
        out_shape=jax.ShapeDtypeStruct((rows, NZ * HEAD), BF16),
        compiler_params=pltpu.CompilerParams(vmem_limit_bytes=VMEM),
        cost_estimate=pl.CostEstimate(flops=ATTEND_COST, bytes_accessed=2_000_000, transcendentals=1_000_000),
    )(lengths, messages)


def output_products(attended, weights):
    rows = attended.shape[0]
    vmem = pl.BlockSpec(memory_space=pltpu.VMEM)
    return pl.pallas_call(
        output_kernel,
        in_specs=[vmem, vmem],
        out_specs=vmem,
        out_shape=jax.ShapeDtypeStruct((4, rows, 256), BF16),
        compiler_params=pltpu.CompilerParams(vmem_limit_bytes=VMEM),
        cost_estimate=pl.CostEstimate(flops=2 * rows * 1024 * 1024, bytes_accessed=5_000_000, transcendentals=0),
    )(attended, weights)


def resid_kernel(p_ref, x_ref, head_ref, resid_ref, stat_ref):
    update = jnp.sum(p_ref[...].astype(F32), axis=0)
    resid = (x_ref[...].astype(F32) + update).astype(BF16)
    resid_ref[...] = resid
    r = resid.astype(F32)
    scores = lax.dot_general(
        head_ref[...], r, NT, precision=lax.Precision.HIGHEST, preferred_element_type=F32
    )
    ones = jnp.ones((8, r.shape[1]), F32)
    squares = lax.dot_general(
        ones, r * r, NT, precision=lax.Precision.HIGHEST, preferred_element_type=F32
    )
    row = lax.broadcasted_iota(jnp.int32, scores.shape, 0)
    stat = jnp.where(row < 6, scores, squares).astype(BF16)
    for k in range(NZ * NYH):
        stat_ref[k] = stat


def resid_and_stats(parts, tokens, heads):
    rows, cols = tokens.shape
    return pl.pallas_call(
        resid_kernel,
        in_specs=[pl.BlockSpec(memory_space=pltpu.VMEM)] * 3,
        out_specs=[pl.BlockSpec(memory_space=pltpu.VMEM)] * 2,
        out_shape=[
            jax.ShapeDtypeStruct((rows, cols), BF16),
            jax.ShapeDtypeStruct((NZ * NYH, 8, rows), BF16),
        ],
        compiler_params=pltpu.CompilerParams(vmem_limit_bytes=VMEM),
        cost_estimate=pl.CostEstimate(flops=2 * rows * cols * 96, bytes_accessed=1_200_000, transcendentals=0),
    )(parts, tokens, heads)


def local(
    tokens,
    row_lengths,
    attn_gain,
    query_weight,
    key_weight,
    value_matrix,
    output_weight,
    final_gain,
    value_head,
):
    rows = tokens.shape[0]
    z, yh, c = lax.axis_index("z"), lax.axis_index("yh"), lax.axis_index("c")
    core = c.astype(jnp.int32)[None]

    xf = tokens.astype(F32)
    gained = (xf * attn_gain[None, :]).astype(BF16)

    first, even = (yh // 2) == 0, (yh % 2) == 0
    with jax.named_scope("weights_yh"):
        kv = lax.ppermute(jnp.concatenate([key_weight.T, value_matrix.T], axis=0), TP, kv_perm())
        q = [query_weight[256 * b : 256 * (b + 1)] for b in range(2)]
        q = [jnp.concatenate([one[:128], one[128:]], axis=1) for one in q]
        q = [jnp.concatenate([q[b], kv[:, 256 * b : 256 * (b + 1)]], axis=0) for b in range(2)]
        q = [
            lax.ppermute(jnp.where(first, q[k], q[1 - k]), ("yh", "c"), head_perm(k))
            for k in range(2)
        ]
        odd = (yh % 2).astype(jnp.int32)[None]
        qkv_send = packed_copies(odd, *q)
    with jax.named_scope("out_yh"):
        o = [output_weight[:128], output_weight[128:]]
        o = [jnp.where(first, o[k], o[1 - k]) for k in range(2)]
        o, qkv_send = lax.optimization_barrier((o, qkv_send))
        o = [lax.ppermute(o[k], ("yh", "c"), head_perm(k)) for k in range(2)]


    swap = [(0, 1), (1, 0)]
    with jax.named_scope("tokens_z"):
        x_all = lax.all_gather(gained, "z", axis=0)
    with jax.named_scope("qkv_rep"):
        qkv_own = lax.all_to_all(qkv_send, ("yl", "x"), 0, 0)
        qkv_other = lax.ppermute(qkv_own, "c", swap)
    with jax.named_scope("out_rep"):
        o, x_all = lax.optimization_barrier((o, x_all))
        out_part = jnp.concatenate([jnp.where(even, o[k], o[1 - k]) for k in range(2)], axis=0)
        out_all = lax.all_gather(out_part, REP, axis=0)
    parts = project(core, x_all, qkv_own, qkv_other, tokens)
    with jax.named_scope("qkv_sum"):
        parts = lax.all_to_all(parts, "yh", 0, 0)
    with jax.named_scope("qkv_z"):
        messages = lax.all_gather(summed(parts), "z", axis=0)
    out_all, messages = lax.optimization_barrier((out_all, messages))
    attended = attend(row_lengths, messages)
    parts = output_products(attended, out_all)
    with jax.named_scope("out_sum"):
        parts = lax.all_to_all(parts, "yh", 0, 0)

    heads = jnp.concatenate([(final_gain[:, None] * value_head).T, jnp.zeros((2, tokens.shape[1]), F32)], axis=0)
    resid_out, stat = resid_and_stats(parts, tokens, heads)

    with jax.named_scope("stat_tp"):
        stat = lax.all_to_all(stat, TP, 0, 0).astype(F32).sum(axis=0)
    logits = stat[:6] * lax.rsqrt(stat[6] / WIDTH + EPS)[None, :]
    position = jnp.arange(rows // row_lengths.shape[0], dtype=jnp.int32)
    live = (position[None, :] < row_lengths[:, None]).reshape(1, rows)
    scores = jnp.where(live, logits, F32(0.0)).T
    return resid_out, scores


def solution(mesh):
    split = Mesh(mesh.devices.reshape(NZ, NYH, NYL, NX, NC), TP + REP)
    in_specs = (
        P(REP, TP),
        P(REP),
        P(TP),
        P(REP, TP),
        P(REP, TP),
        P(REP, TP),
        P(REP, TP),
        P(TP),
        P(TP, None),
    )
    out_specs = (P(REP, TP), P(REP, None))
    return jax.shard_map(local, mesh=split, in_specs=in_specs, out_specs=out_specs, check_vma=False)
```

```python
import jax
import jax.numpy as jnp
from jax import lax
from jax.experimental import pallas as pl
from jax.experimental.pallas import tpu as pltpu
from jax.sharding import Mesh
from jax.sharding import PartitionSpec as P

HEAD = 128
EPS = 1e-05
WIDTH = 8192
NZ, NYH, NYL, NX, NC = 8, 4, 2, 4, 2
TP = ("z", "yh")
REP = ("yl", "x", "c")
VMEM = 48 * 1024 * 1024
F32 = jnp.float32
BF16 = jnp.bfloat16
NT = (((1,), (1,)), ((), ()))
OWN_COST = 30_000_000_000
ATTEND_COST = 8_000_000_000


def copies(x, axis, count):
    return lax.all_to_all(jnp.broadcast_to(x[None], (count, *x.shape)), axis, 0, 0)


def head_perm(k):
    pairs = []
    for yh in range(NYH):
        for c in range(NC):
            b = (yh // 2 + k) % 2
            pairs.append((yh * NC + c, (2 * c + b) * NC + yh % 2))
    return pairs


def kv_perm():
    return [
        (z * NYH + yh, ((z % 2) * 4 + yh) * NYH + z // 2) for z in range(NZ) for yh in range(NYH)
    ]


def split_sum(total):
    high = total.astype(BF16)
    low = (total - high.astype(F32)).astype(BF16)
    return high, low


def pack_kernel(odd_ref, q0, q1, out_ref):
    even = odd_ref[0] == 0
    first, second = jnp.where(even, q0[...], q1[...]), jnp.where(even, q1[...], q0[...])
    whole = jnp.concatenate([first[:128], second[:128], first[128:], second[128:]], axis=0)
    for k in range(NYL * NX):
        out_ref[k] = whole


def packed_copies(odd, *parts):
    vmem = pl.BlockSpec(memory_space=pltpu.VMEM)
    return pl.pallas_call(
        pack_kernel,
        in_specs=[pl.BlockSpec(memory_space=pltpu.SMEM)] + [vmem] * 2,
        out_specs=vmem,
        out_shape=jax.ShapeDtypeStruct((NYL * NX, 320, 256), BF16),
        compiler_params=pltpu.CompilerParams(vmem_limit_bytes=VMEM),
        cost_estimate=pl.CostEstimate(flops=1000, bytes_accessed=1000, transcendentals=0),
    )(odd, *parts)


def columns(w_ref, hi):
    return jnp.concatenate(
        [
            w_ref[k, hi * 128 : (hi + 1) * 128, half * 128 : (half + 1) * 128]
            for k in range(NZ)
            for half in range(2)
        ],
        axis=0,
    )


def project_side(x_ref, w_ref, stat, out_ref, d):
    rows = x_ref.shape[1]
    x = jnp.concatenate([x_ref[k] for k in range(NZ)], axis=1)
    w = jnp.concatenate([columns(w_ref, hi) for hi in range(2)], axis=1)
    q = jnp.dot(x, w, preferred_element_type=F32).astype(BF16)
    kvw = jnp.concatenate([w_ref[k, 256:320, :] for k in range(NZ)], axis=1)
    kv = lax.dot_general(kvw, x, NT, preferred_element_type=F32).astype(BF16)
    for hi in range(2):
        out_ref[2 * hi + d, 0:rows, :] = q[:, hi * 128 : (hi + 1) * 128]
        for p in range(3):
            at = rows + 32 * p
            out_ref[2 * hi + d, at : at + 32, :] = kv[hi * 32 : (hi + 1) * 32, 128 * p : 128 * (p + 1)]
        out_ref[2 * hi + d, rows + 96 : rows + 112, :] = stat


def row_squares(t):
    sq = t.astype(F32) * t.astype(F32)
    high, low = split_sum(sq)
    ones = jnp.ones((16, t.shape[1]), BF16)
    total = lax.dot_general(ones, high, NT, preferred_element_type=F32)
    return total + lax.dot_general(ones, low, NT, preferred_element_type=F32)


def stat_rows(sums):
    pairs = [half for one in sums for half in split_sum(one)]
    return jnp.concatenate(pairs + [jnp.zeros((10, 128), BF16)], axis=0)


def own_kernel(core_ref, x_ref, w_ref, tokens_ref, out_ref):
    sq = row_squares(tokens_ref[...])
    stat = stat_rows([sq[0:1, 128 * p : 128 * (p + 1)] for p in range(3)])
    project_side(x_ref, w_ref, stat, out_ref, core_ref[0])


def other_kernel(core_ref, x_ref, w_ref, first_ref, out_ref):
    core = core_ref[0]
    rows = x_ref.shape[1]
    for hi in range(2):
        out_ref[2 * hi + core] = first_ref[2 * hi + core]
    project_side(x_ref, w_ref, first_ref[core, rows + 96 : rows + 112, :], out_ref, 1 - core)


def project(core, x, own, other, tokens):
    rows = x.shape[1]
    vmem = pl.BlockSpec(memory_space=pltpu.VMEM)
    smem = pl.BlockSpec(memory_space=pltpu.SMEM)

    def call(kernel, flops, *args):
        return pl.pallas_call(
            kernel,
            in_specs=[smem] + [vmem] * (len(args) - 1),
            out_specs=vmem,
            out_shape=jax.ShapeDtypeStruct((4, rows + 112, 128), BF16),
            compiler_params=pltpu.CompilerParams(vmem_limit_bytes=VMEM),
            cost_estimate=pl.CostEstimate(flops=flops, bytes_accessed=3_000_000, transcendentals=0),
        )(*args)

    first = call(own_kernel, OWN_COST, core, x, own, tokens)
    return call(other_kernel, 2 * rows * 2048 * 320, core, x, other, first)


def sum_kernel(p_ref, out_ref):
    rows = p_ref.shape[1] - 112
    total = jnp.sum(p_ref[...].astype(F32), axis=0)
    out_ref[0 : rows + 96, :] = total[0 : rows + 96].astype(BF16)
    at = rows + 96
    sums = [total[at + 2 * p : at + 2 * p + 1] + total[at + 2 * p + 1 : at + 2 * p + 2] for p in range(3)]
    out_ref[at : at + 16, :] = stat_rows(sums)


def summed(parts):
    return pl.pallas_call(
        sum_kernel,
        in_specs=[pl.BlockSpec(memory_space=pltpu.VMEM)],
        out_specs=pl.BlockSpec(memory_space=pltpu.VMEM),
        out_shape=jax.ShapeDtypeStruct(parts.shape[1:], BF16),
        compiler_params=pltpu.CompilerParams(vmem_limit_bytes=VMEM),
    )(parts)


def attend_kernel(len_ref, m_ref, att_ref):
    rows = m_ref.shape[1] - 112
    half = rows // 2
    at = [rows + 32 * p for p in range(3)]
    stats = jnp.sum(m_ref[:, rows + 96 : rows + 112, :].astype(F32), axis=0)
    stats = jnp.concatenate(
        [stats[2 * p : 2 * p + 1] + stats[2 * p + 1 : 2 * p + 2] for p in range(3)], axis=1
    )
    scale = lax.rsqrt(stats * (1.0 / WIDTH) + EPS)
    wide = jnp.broadcast_to(scale, (HEAD, rows))
    key = jnp.concatenate([m_ref[:, a : a + 16, :].reshape(HEAD, 128) for a in at], axis=1)
    key = (key.astype(F32) * wide).astype(BF16)
    value = jnp.concatenate([m_ref[:, a + 16 : a + 32, :].reshape(HEAD, 128) for a in at], axis=1)
    value = (value.astype(F32) * wide).astype(BF16)
    column = wide.T[:, 0:1] * (1.0 / HEAD**0.5)
    for seq in range(2):
        first = seq * 128
        k = key[:, first : first + 256]
        v = value[:, first : first + 256]
        i = lax.broadcasted_iota(jnp.int32, (half, 256), 0)
        j = lax.broadcasted_iota(jnp.int32, (half, 256), 1) - (seq * half - first)
        allowed = (j >= 0) & (j <= i) & (j < len_ref[seq])
        c = column[seq * half : (seq + 1) * half]
        for head in range(NZ):
            q = m_ref[head, seq * half : (seq + 1) * half, :]
            scores = jnp.dot(q, k, preferred_element_type=F32) * c
            scores = jnp.where(allowed, scores, F32(-1e30))
            scores = scores - jnp.max(scores, axis=1, keepdims=True)
            expo = jnp.exp(scores)
            probs = (expo * (1.0 / jnp.sum(expo, axis=1, keepdims=True))).astype(BF16)
            o = lax.dot_general(probs, v, NT, preferred_element_type=F32)
            att_ref[seq * half : (seq + 1) * half, head * 128 : (head + 1) * 128] = o.astype(BF16)


def output_kernel(att_ref, w_ref, out_ref):
    a = att_ref[...]
    for d in range(2):
        for hi in range(2):
            w = jnp.concatenate(
                [w_ref[2 * k + d, hi * 128 : (hi + 1) * 128] for k in range(NZ)], axis=0
            )
            out_ref[2 * hi + d] = jnp.dot(a, w, preferred_element_type=F32).astype(BF16)


def attend(lengths, messages):
    rows = messages.shape[1] - 112
    vmem = pl.BlockSpec(memory_space=pltpu.VMEM)
    smem = pl.BlockSpec(memory_space=pltpu.SMEM)
    return pl.pallas_call(
        attend_kernel,
        in_specs=[smem, vmem],
        out_specs=vmem,
        out_shape=jax.ShapeDtypeStruct((rows, NZ * HEAD), BF16),
        compiler_params=pltpu.CompilerParams(vmem_limit_bytes=VMEM),
        cost_estimate=pl.CostEstimate(flops=ATTEND_COST, bytes_accessed=2_000_000, transcendentals=1_000_000),
    )(lengths, messages)


def output_products(attended, weights):
    rows = attended.shape[0]
    vmem = pl.BlockSpec(memory_space=pltpu.VMEM)
    return pl.pallas_call(
        output_kernel,
        in_specs=[vmem, vmem],
        out_specs=vmem,
        out_shape=jax.ShapeDtypeStruct((4, rows, 256), BF16),
        compiler_params=pltpu.CompilerParams(vmem_limit_bytes=VMEM),
        cost_estimate=pl.CostEstimate(flops=2 * rows * 1024 * 1024, bytes_accessed=5_000_000, transcendentals=0),
    )(attended, weights)


def resid_kernel(p_ref, x_ref, head_ref, resid_ref, stat_ref):
    update = jnp.sum(p_ref[...].astype(F32), axis=0)
    resid = (x_ref[...].astype(F32) + update).astype(BF16)
    resid_ref[...] = resid
    head = head_ref[...]
    h1 = head.astype(BF16)
    h2 = (head - h1.astype(F32)).astype(BF16)
    h3 = (head - h1.astype(F32) - h2.astype(F32)).astype(BF16)
    scores = sum(
        lax.dot_general(h, resid, NT, preferred_element_type=F32) for h in (h3, h2, h1)
    )
    row = lax.broadcasted_iota(jnp.int32, scores.shape, 0)
    stat = jnp.where(row < 6, scores, row_squares(resid)[0:8]).astype(BF16)
    for k in range(NZ * NYH):
        stat_ref[k] = stat


def resid_and_stats(parts, tokens, heads):
    rows, cols = tokens.shape
    return pl.pallas_call(
        resid_kernel,
        in_specs=[pl.BlockSpec(memory_space=pltpu.VMEM)] * 3,
        out_specs=[pl.BlockSpec(memory_space=pltpu.VMEM)] * 2,
        out_shape=[
            jax.ShapeDtypeStruct((rows, cols), BF16),
            jax.ShapeDtypeStruct((NZ * NYH, 8, rows), BF16),
        ],
        compiler_params=pltpu.CompilerParams(vmem_limit_bytes=VMEM),
        cost_estimate=pl.CostEstimate(flops=2 * rows * cols * 96, bytes_accessed=1_200_000, transcendentals=0),
    )(parts, tokens, heads)


def local(
    tokens,
    row_lengths,
    attn_gain,
    query_weight,
    key_weight,
    value_matrix,
    output_weight,
    final_gain,
    value_head,
):
    rows = tokens.shape[0]
    z, yh, c = lax.axis_index("z"), lax.axis_index("yh"), lax.axis_index("c")
    core = c.astype(jnp.int32)[None]

    xf = tokens.astype(F32)
    gained = (xf * attn_gain[None, :]).astype(BF16)

    first, even = (yh // 2) == 0, (yh % 2) == 0
    with jax.named_scope("weights_yh"):
        kv = lax.ppermute(jnp.concatenate([key_weight.T, value_matrix.T], axis=0), TP, kv_perm())
        q = [query_weight[256 * b : 256 * (b + 1)] for b in range(2)]
        q = [jnp.concatenate([one[:128], one[128:]], axis=1) for one in q]
        q = [jnp.concatenate([q[b], kv[:, 256 * b : 256 * (b + 1)]], axis=0) for b in range(2)]
        q = [
            lax.ppermute(jnp.where(first, q[k], q[1 - k]), ("yh", "c"), head_perm(k))
            for k in range(2)
        ]
        odd = (yh % 2).astype(jnp.int32)[None]
        qkv_send = packed_copies(odd, *q)
    with jax.named_scope("out_yh"):
        o = [output_weight[:128], output_weight[128:]]
        o = [jnp.where(first, o[k], o[1 - k]) for k in range(2)]
        o, qkv_send = lax.optimization_barrier((o, qkv_send))
        o = [lax.ppermute(o[k], ("yh", "c"), head_perm(k)) for k in range(2)]


    swap = [(0, 1), (1, 0)]
    with jax.named_scope("tokens_z"):
        x_all = lax.all_gather(gained, "z", axis=0)
    with jax.named_scope("qkv_rep"):
        qkv_own = lax.all_to_all(qkv_send, ("yl", "x"), 0, 0)
        qkv_other = lax.ppermute(qkv_own, "c", swap)
    with jax.named_scope("out_rep"):
        o, x_all = lax.optimization_barrier((o, x_all))
        out_part = jnp.concatenate([jnp.where(even, o[k], o[1 - k]) for k in range(2)], axis=0)
        out_all = lax.all_gather(out_part, REP, axis=0)
    parts = project(core, x_all, qkv_own, qkv_other, tokens)
    with jax.named_scope("qkv_sum"):
        parts = lax.all_to_all(parts, "yh", 0, 0)
    with jax.named_scope("qkv_z"):
        messages = lax.all_gather(summed(parts), "z", axis=0)
    out_all, messages = lax.optimization_barrier((out_all, messages))
    attended = attend(row_lengths, messages)
    parts = output_products(attended, out_all)
    with jax.named_scope("out_sum"):
        parts = lax.all_to_all(parts, "yh", 0, 0)

    heads = jnp.concatenate([(final_gain[:, None] * value_head).T, jnp.zeros((2, tokens.shape[1]), F32)], axis=0)
    resid_out, stat = resid_and_stats(parts, tokens, heads)

    with jax.named_scope("stat_tp"):
        stat = lax.all_to_all(stat, TP, 0, 0).astype(F32).sum(axis=0)
    logits = stat[:6] * lax.rsqrt(stat[6] / WIDTH + EPS)[None, :]
    position = jnp.arange(rows // row_lengths.shape[0], dtype=jnp.int32)
    live = (position[None, :] < row_lengths[:, None]).reshape(1, rows)
    scores = jnp.where(live, logits, F32(0.0)).T
    return resid_out, scores


def solution(mesh):
    split = Mesh(mesh.devices.reshape(NZ, NYH, NYL, NX, NC), TP + REP)
    in_specs = (
        P(REP, TP),
        P(REP),
        P(TP),
        P(REP, TP),
        P(REP, TP),
        P(REP, TP),
        P(REP, TP),
        P(TP),
        P(TP, None),
    )
    out_specs = (P(REP, TP), P(REP, None))
    return jax.shard_map(local, mesh=split, in_specs=in_specs, out_specs=out_specs, check_vma=False)
```

```python
import jax
import jax.numpy as jnp
from jax import lax
from jax.experimental import pallas as pl
from jax.experimental.pallas import tpu as pltpu
from jax.sharding import Mesh
from jax.sharding import PartitionSpec as P

HEAD = 128
EPS = 1e-05
WIDTH = 8192
NZ, NYH, NYL, NX, NC = 8, 4, 2, 4, 2
TP = ("z", "yh")
REP = ("yl", "x", "c")
VMEM = 48 * 1024 * 1024
F32 = jnp.float32
BF16 = jnp.bfloat16
NT = (((1,), (1,)), ((), ()))
OWN_COST = 30_000_000_000
ATTEND_COST = 8_000_000_000


def copies(x, axis, count):
    return lax.all_to_all(jnp.broadcast_to(x[None], (count, *x.shape)), axis, 0, 0)


def head_perm(k):
    pairs = []
    for yh in range(NYH):
        for c in range(NC):
            b = (yh // 2 + k) % 2
            pairs.append((yh * NC + c, (2 * c + b) * NC + yh % 2))
    return pairs


def kv_perm():
    return [
        (z * NYH + yh, ((z % 2) * 4 + yh) * NYH + z // 2) for z in range(NZ) for yh in range(NYH)
    ]


def split_sum(total):
    high = total.astype(BF16)
    low = (total - high.astype(F32)).astype(BF16)
    return high, low


def pack_kernel(odd_ref, q0, q1, kv0, kv1, out_ref):
    even = odd_ref[0] == 0
    q, kv = (q0[...], q1[...]), (kv0[...], kv1[...])
    whole = jnp.concatenate(
        [jnp.where(even, a[k], a[1 - k]) for a in (q, kv) for k in range(2)], axis=0
    )
    for k in range(NYL * NX):
        out_ref[k] = whole


def packed_copies(odd, *parts):
    vmem = pl.BlockSpec(memory_space=pltpu.VMEM)
    return pl.pallas_call(
        pack_kernel,
        in_specs=[pl.BlockSpec(memory_space=pltpu.SMEM)] + [vmem] * 4,
        out_specs=vmem,
        out_shape=jax.ShapeDtypeStruct((NYL * NX, 320, 256), BF16),
        compiler_params=pltpu.CompilerParams(vmem_limit_bytes=VMEM),
        cost_estimate=pl.CostEstimate(flops=1000, bytes_accessed=1000, transcendentals=0),
    )(odd, *parts)


def columns(w_ref, hi):
    return jnp.concatenate(
        [
            w_ref[k, hi * 128 : (hi + 1) * 128, half * 128 : (half + 1) * 128]
            for k in range(NZ)
            for half in range(2)
        ],
        axis=0,
    )


def project_side(x_ref, w_ref, stat, out_ref, d):
    rows = x_ref.shape[1]
    x = jnp.concatenate([x_ref[k] for k in range(NZ)], axis=1)
    w = jnp.concatenate([columns(w_ref, hi) for hi in range(2)], axis=1)
    q = jnp.dot(x, w, preferred_element_type=F32).astype(BF16)
    kvw = jnp.concatenate([w_ref[k, 256:320, :] for k in range(NZ)], axis=1)
    kv = lax.dot_general(kvw, x, NT, preferred_element_type=F32).astype(BF16)
    for hi in range(2):
        out_ref[2 * hi + d, 0:rows, :] = q[:, hi * 128 : (hi + 1) * 128]
        for p in range(3):
            at = rows + 32 * p
            out_ref[2 * hi + d, at : at + 32, :] = kv[hi * 32 : (hi + 1) * 32, 128 * p : 128 * (p + 1)]
        out_ref[2 * hi + d, rows + 96 : rows + 112, :] = stat


def row_squares(t):
    sq = t.astype(F32) * t.astype(F32)
    high, low = split_sum(sq)
    ones = jnp.ones((16, t.shape[1]), BF16)
    total = lax.dot_general(ones, high, NT, preferred_element_type=F32)
    return total + lax.dot_general(ones, low, NT, preferred_element_type=F32)


def stat_rows(sums):
    pairs = [half for one in sums for half in split_sum(one)]
    return jnp.concatenate(pairs + [jnp.zeros((10, 128), BF16)], axis=0)


def own_kernel(core_ref, x_ref, w_ref, tokens_ref, out_ref):
    sq = row_squares(tokens_ref[...])
    stat = stat_rows([sq[0:1, 128 * p : 128 * (p + 1)] for p in range(3)])
    project_side(x_ref, w_ref, stat, out_ref, core_ref[0])


def other_kernel(core_ref, x_ref, w_ref, first_ref, o0_ref, o1_ref, out_ref, o_ref):
    even = core_ref[1] == 0
    o_ref[0:128, :] = jnp.where(even, o0_ref[...], o1_ref[...])
    o_ref[128:256, :] = jnp.where(even, o1_ref[...], o0_ref[...])
    core = core_ref[0]
    rows = x_ref.shape[1]
    for hi in range(2):
        out_ref[2 * hi + core] = first_ref[2 * hi + core]
    project_side(x_ref, w_ref, first_ref[core, rows + 96 : rows + 112, :], out_ref, 1 - core)


def project(core, x, own, other, tokens, out_blocks):
    rows = x.shape[1]
    vmem = pl.BlockSpec(memory_space=pltpu.VMEM)
    smem = pl.BlockSpec(memory_space=pltpu.SMEM)

    def call(kernel, flops, more, *args):
        return pl.pallas_call(
            kernel,
            in_specs=[smem] + [vmem] * (len(args) - 1),
            out_specs=[vmem] * (1 + len(more)),
            out_shape=[jax.ShapeDtypeStruct((4, rows + 112, 128), BF16)] + more,
            compiler_params=pltpu.CompilerParams(vmem_limit_bytes=VMEM),
            cost_estimate=pl.CostEstimate(flops=flops, bytes_accessed=3_000_000, transcendentals=0),
        )(*args)

    (first,) = call(own_kernel, OWN_COST, [], core, x, own, tokens)
    joined = jax.ShapeDtypeStruct((256, 256), BF16)
    cost = 2 * rows * 2048 * 320
    return call(other_kernel, cost, [joined], core, x, other, first, *out_blocks)


def sum_kernel(p_ref, out_ref):
    rows = p_ref.shape[1] - 112
    total = jnp.sum(p_ref[...].astype(F32), axis=0)
    out_ref[0 : rows + 96, :] = total[0 : rows + 96].astype(BF16)
    at = rows + 96
    sums = [total[at + 2 * p : at + 2 * p + 1] + total[at + 2 * p + 1 : at + 2 * p + 2] for p in range(3)]
    out_ref[at : at + 16, :] = stat_rows(sums)


def summed(parts):
    return pl.pallas_call(
        sum_kernel,
        in_specs=[pl.BlockSpec(memory_space=pltpu.VMEM)],
        out_specs=pl.BlockSpec(memory_space=pltpu.VMEM),
        out_shape=jax.ShapeDtypeStruct(parts.shape[1:], BF16),
        compiler_params=pltpu.CompilerParams(vmem_limit_bytes=VMEM),
    )(parts)


def attend_kernel(len_ref, m_ref, att_ref):
    rows = m_ref.shape[1] - 112
    half = rows // 2
    at = [rows + 32 * p for p in range(3)]
    stats = jnp.sum(m_ref[:, rows + 96 : rows + 112, :].astype(F32), axis=0)
    stats = jnp.concatenate(
        [stats[2 * p : 2 * p + 1] + stats[2 * p + 1 : 2 * p + 2] for p in range(3)], axis=1
    )
    scale = lax.rsqrt(stats * (1.0 / WIDTH) + EPS)
    wide = jnp.broadcast_to(scale, (HEAD, rows))
    key = jnp.concatenate([m_ref[:, a : a + 16, :].reshape(HEAD, 128) for a in at], axis=1)
    key = (key.astype(F32) * wide).astype(BF16)
    value = jnp.concatenate([m_ref[:, a + 16 : a + 32, :].reshape(HEAD, 128) for a in at], axis=1)
    value = (value.astype(F32) * wide).astype(BF16)
    column = wide.T[:, 0:1] * (1.0 / HEAD**0.5)
    for seq in range(2):
        first = seq * 128
        k = key[:, first : first + 256]
        v = value[:, first : first + 256]
        i = lax.broadcasted_iota(jnp.int32, (half, 256), 0)
        j = lax.broadcasted_iota(jnp.int32, (half, 256), 1) - (seq * half - first)
        allowed = (j >= 0) & (j <= i) & (j < len_ref[seq])
        c = column[seq * half : (seq + 1) * half]
        for head in range(NZ):
            q = m_ref[head, seq * half : (seq + 1) * half, :]
            scores = jnp.dot(q, k, preferred_element_type=F32) * c
            scores = jnp.where(allowed, scores, F32(-1e30))
            scores = scores - jnp.max(scores, axis=1, keepdims=True)
            expo = jnp.exp(scores)
            probs = (expo * (1.0 / jnp.sum(expo, axis=1, keepdims=True))).astype(BF16)
            o = lax.dot_general(probs, v, NT, preferred_element_type=F32)
            att_ref[seq * half : (seq + 1) * half, head * 128 : (head + 1) * 128] = o.astype(BF16)


def output_kernel(att_ref, w_ref, out_ref):
    a = att_ref[...]
    for d in range(2):
        for hi in range(2):
            w = jnp.concatenate(
                [w_ref[2 * k + d, hi * 128 : (hi + 1) * 128] for k in range(NZ)], axis=0
            )
            out_ref[2 * hi + d] = jnp.dot(a, w, preferred_element_type=F32).astype(BF16)


def attend(lengths, messages):
    rows = messages.shape[1] - 112
    vmem = pl.BlockSpec(memory_space=pltpu.VMEM)
    smem = pl.BlockSpec(memory_space=pltpu.SMEM)
    return pl.pallas_call(
        attend_kernel,
        in_specs=[smem, vmem],
        out_specs=vmem,
        out_shape=jax.ShapeDtypeStruct((rows, NZ * HEAD), BF16),
        compiler_params=pltpu.CompilerParams(vmem_limit_bytes=VMEM),
        cost_estimate=pl.CostEstimate(flops=ATTEND_COST, bytes_accessed=2_000_000, transcendentals=1_000_000),
    )(lengths, messages)


def output_products(attended, weights):
    rows = attended.shape[0]
    vmem = pl.BlockSpec(memory_space=pltpu.VMEM)
    return pl.pallas_call(
        output_kernel,
        in_specs=[vmem, vmem],
        out_specs=vmem,
        out_shape=jax.ShapeDtypeStruct((4, rows, 256), BF16),
        compiler_params=pltpu.CompilerParams(vmem_limit_bytes=VMEM),
        cost_estimate=pl.CostEstimate(flops=2 * rows * 1024 * 1024, bytes_accessed=5_000_000, transcendentals=0),
    )(attended, weights)


def resid_kernel(p_ref, x_ref, head_ref, resid_ref, stat_ref):
    update = jnp.sum(p_ref[...].astype(F32), axis=0)
    resid = (x_ref[...].astype(F32) + update).astype(BF16)
    resid_ref[...] = resid
    head = head_ref[...]
    h1 = head.astype(BF16)
    h2 = (head - h1.astype(F32)).astype(BF16)
    h3 = (head - h1.astype(F32) - h2.astype(F32)).astype(BF16)
    scores = sum(
        lax.dot_general(h, resid, NT, preferred_element_type=F32) for h in (h3, h2, h1)
    )
    row = lax.broadcasted_iota(jnp.int32, scores.shape, 0)
    stat = jnp.where(row < 6, scores, row_squares(resid)[0:8]).astype(BF16)
    for k in range(NZ * NYH):
        stat_ref[k] = stat


def resid_and_stats(parts, tokens, heads):
    rows, cols = tokens.shape
    return pl.pallas_call(
        resid_kernel,
        in_specs=[pl.BlockSpec(memory_space=pltpu.VMEM)] * 3,
        out_specs=[pl.BlockSpec(memory_space=pltpu.VMEM)] * 2,
        out_shape=[
            jax.ShapeDtypeStruct((rows, cols), BF16),
            jax.ShapeDtypeStruct((NZ * NYH, 8, rows), BF16),
        ],
        compiler_params=pltpu.CompilerParams(vmem_limit_bytes=VMEM),
        cost_estimate=pl.CostEstimate(flops=2 * rows * cols * 96, bytes_accessed=1_200_000, transcendentals=0),
    )(parts, tokens, heads)


def local(
    tokens,
    row_lengths,
    attn_gain,
    query_weight,
    key_weight,
    value_matrix,
    output_weight,
    final_gain,
    value_head,
):
    rows = tokens.shape[0]
    z, yh, c = lax.axis_index("z"), lax.axis_index("yh"), lax.axis_index("c")
    core = jnp.stack([c, yh % 2]).astype(jnp.int32)

    xf = tokens.astype(F32)
    gained = (xf * attn_gain[None, :]).astype(BF16)

    first, even = (yh // 2) == 0, (yh % 2) == 0
    with jax.named_scope("weights_yh"):
        kv = lax.ppermute(jnp.concatenate([key_weight.T, value_matrix.T], axis=0), TP, kv_perm())
        q = [query_weight[256 * b : 256 * (b + 1)] for b in range(2)]
        q = [jnp.concatenate([one[:128], one[128:]], axis=1) for one in q]
        q = [
            lax.ppermute(jnp.where(first, q[k], q[1 - k]), ("yh", "c"), head_perm(k))
            for k in range(2)
        ]
        kv = [kv[:, :256], kv[:, 256:]]
        kv = [
            lax.ppermute(jnp.where(first, kv[k], kv[1 - k]), ("yh", "c"), head_perm(k))
            for k in range(2)
        ]
        odd = (yh % 2).astype(jnp.int32)[None]
        qkv_send = packed_copies(odd, *q, *kv)
    with jax.named_scope("out_yh"):
        o = [output_weight[:128], output_weight[128:]]
        o = [jnp.where(first, o[k], o[1 - k]) for k in range(2)]
        o, qkv_send = lax.optimization_barrier((o, qkv_send))
        o = [lax.ppermute(o[k], ("yh", "c"), head_perm(k)) for k in range(2)]


    swap = [(0, 1), (1, 0)]
    with jax.named_scope("tokens_z"):
        x_all = lax.all_gather(gained, "z", axis=0)
    with jax.named_scope("qkv_rep"):
        qkv_own = lax.all_to_all(qkv_send, ("yl", "x"), 0, 0)
        qkv_other = lax.ppermute(qkv_own, "c", swap)
    parts, out_part = project(core, x_all, qkv_own, qkv_other, tokens, o)
    with jax.named_scope("out_rep"):
        out_all = lax.all_gather(out_part, REP, axis=0)
    with jax.named_scope("qkv_sum"):
        parts = lax.all_to_all(parts, "yh", 0, 0)
    with jax.named_scope("qkv_z"):
        messages = lax.all_gather(summed(parts), "z", axis=0)
    out_all, messages = lax.optimization_barrier((out_all, messages))
    attended = attend(row_lengths, messages)
    parts = output_products(attended, out_all)
    with jax.named_scope("out_sum"):
        parts = lax.all_to_all(parts, "yh", 0, 0)

    heads = jnp.concatenate([(final_gain[:, None] * value_head).T, jnp.zeros((2, tokens.shape[1]), F32)], axis=0)
    resid_out, stat = resid_and_stats(parts, tokens, heads)

    with jax.named_scope("stat_tp"):
        stat = lax.all_to_all(stat, TP, 0, 0).astype(F32).sum(axis=0)
    logits = stat[:6] * lax.rsqrt(stat[6] / WIDTH + EPS)[None, :]
    position = jnp.arange(rows // row_lengths.shape[0], dtype=jnp.int32)
    live = (position[None, :] < row_lengths[:, None]).reshape(1, rows)
    scores = jnp.where(live, logits, F32(0.0)).T
    return resid_out, scores


def solution(mesh):
    split = Mesh(mesh.devices.reshape(NZ, NYH, NYL, NX, NC), TP + REP)
    in_specs = (
        P(REP, TP),
        P(REP),
        P(TP),
        P(REP, TP),
        P(REP, TP),
        P(REP, TP),
        P(REP, TP),
        P(TP),
        P(TP, None),
    )
    out_specs = (P(REP, TP), P(REP, None))
    return jax.shard_map(local, mesh=split, in_specs=in_specs, out_specs=out_specs, check_vma=False)
```

```python
import jax
import jax.numpy as jnp
from jax import lax
from jax.experimental import pallas as pl
from jax.experimental.pallas import tpu as pltpu
from jax.sharding import Mesh
from jax.sharding import PartitionSpec as P

HEAD = 128
EPS = 1e-05
WIDTH = 8192
NZ, NYH, NYL, NX, NC = 8, 4, 2, 4, 2
TP = ("z", "yh")
REP = ("yl", "x", "c")
VMEM = 48 * 1024 * 1024
F32 = jnp.float32
BF16 = jnp.bfloat16
NT = (((1,), (1,)), ((), ()))
OWN_COST = 30_000_000_000
ATTEND_COST = 8_000_000_000


def copies(x, axis, count):
    return lax.all_to_all(jnp.broadcast_to(x[None], (count, *x.shape)), axis, 0, 0)


def head_perm(k):
    pairs = []
    for yh in range(NYH):
        for c in range(NC):
            b = (yh // 2 + k) % 2
            pairs.append((yh * NC + c, (2 * c + b) * NC + yh % 2))
    return pairs


def kv_perm():
    return [
        (z * NYH + yh, ((z % 2) * 4 + yh) * NYH + z // 2) for z in range(NZ) for yh in range(NYH)
    ]


def split_sum(total):
    high = total.astype(BF16)
    low = (total - high.astype(F32)).astype(BF16)
    return high, low


def pack_kernel(odd_ref, q0, q1, kv0, kv1, out_ref):
    even = odd_ref[0] == 0
    q, kv = (q0[...], q1[...]), (kv0[...], kv1[...])
    whole = jnp.concatenate(
        [jnp.where(even, a[k], a[1 - k]) for a in (q, kv) for k in range(2)], axis=0
    )
    for k in range(NYL * NX):
        out_ref[k] = whole


def packed_copies(odd, *parts):
    vmem = pl.BlockSpec(memory_space=pltpu.VMEM)
    return pl.pallas_call(
        pack_kernel,
        in_specs=[pl.BlockSpec(memory_space=pltpu.SMEM)] + [vmem] * 4,
        out_specs=vmem,
        out_shape=jax.ShapeDtypeStruct((NYL * NX, 320, 256), BF16),
        compiler_params=pltpu.CompilerParams(vmem_limit_bytes=VMEM),
        cost_estimate=pl.CostEstimate(flops=1000, bytes_accessed=1000, transcendentals=0),
    )(odd, *parts)


def columns(w_ref, hi):
    return jnp.concatenate(
        [
            w_ref[k, hi * 128 : (hi + 1) * 128, half * 128 : (half + 1) * 128]
            for k in range(NZ)
            for half in range(2)
        ],
        axis=0,
    )


def project_side(x_ref, w_ref, stat, out_ref, d):
    rows = x_ref.shape[1]
    x = jnp.concatenate([x_ref[k] for k in range(NZ)], axis=1)
    w = jnp.concatenate([columns(w_ref, hi) for hi in range(2)], axis=1)
    q = jnp.dot(x, w, preferred_element_type=F32).astype(BF16)
    kvw = jnp.concatenate([w_ref[k, 256:320, :] for k in range(NZ)], axis=1)
    kv = lax.dot_general(kvw, x, NT, preferred_element_type=F32).astype(BF16)
    for hi in range(2):
        out_ref[2 * hi + d, 0:rows, :] = q[:, hi * 128 : (hi + 1) * 128]
        for p in range(3):
            at = rows + 32 * p
            out_ref[2 * hi + d, at : at + 32, :] = kv[hi * 32 : (hi + 1) * 32, 128 * p : 128 * (p + 1)]
        out_ref[2 * hi + d, rows + 96 : rows + 112, :] = stat


def row_squares(t):
    sq = t.astype(F32) * t.astype(F32)
    high, low = split_sum(sq)
    ones = jnp.ones((16, t.shape[1]), BF16)
    total = lax.dot_general(ones, high, NT, preferred_element_type=F32)
    return total + lax.dot_general(ones, low, NT, preferred_element_type=F32)


def stat_rows(sums):
    pairs = [half for one in sums for half in split_sum(one)]
    return jnp.concatenate(pairs + [jnp.zeros((10, 128), BF16)], axis=0)


def own_kernel(core_ref, x_ref, w_ref, tokens_ref, out_ref):
    sq = row_squares(tokens_ref[...])
    stat = stat_rows([sq[0:1, 128 * p : 128 * (p + 1)] for p in range(3)])
    project_side(x_ref, w_ref, stat, out_ref, core_ref[0])


def other_kernel(core_ref, x_ref, w_ref, first_ref, out_ref):
    core = core_ref[0]
    rows = x_ref.shape[1]
    for hi in range(2):
        out_ref[2 * hi + core] = first_ref[2 * hi + core]
    project_side(x_ref, w_ref, first_ref[core, rows + 96 : rows + 112, :], out_ref, 1 - core)


def project(core, x, own, other, tokens):
    rows = x.shape[1]
    vmem = pl.BlockSpec(memory_space=pltpu.VMEM)
    smem = pl.BlockSpec(memory_space=pltpu.SMEM)

    def call(kernel, flops, *args):
        return pl.pallas_call(
            kernel,
            in_specs=[smem] + [vmem] * (len(args) - 1),
            out_specs=vmem,
            out_shape=jax.ShapeDtypeStruct((4, rows + 112, 128), BF16),
            compiler_params=pltpu.CompilerParams(vmem_limit_bytes=VMEM),
            cost_estimate=pl.CostEstimate(flops=flops, bytes_accessed=3_000_000, transcendentals=0),
        )(*args)

    first = call(own_kernel, OWN_COST, core, x, own, tokens)
    return call(other_kernel, 2 * rows * 2048 * 320, core, x, other, first)


def sum_kernel(p_ref, out_ref):
    rows = p_ref.shape[1] - 112
    total = jnp.sum(p_ref[...].astype(F32), axis=0)
    out_ref[0 : rows + 96, :] = total[0 : rows + 96].astype(BF16)
    at = rows + 96
    sums = [total[at + 2 * p : at + 2 * p + 1] + total[at + 2 * p + 1 : at + 2 * p + 2] for p in range(3)]
    out_ref[at : at + 16, :] = stat_rows(sums)


def summed(parts):
    return pl.pallas_call(
        sum_kernel,
        in_specs=[pl.BlockSpec(memory_space=pltpu.VMEM)],
        out_specs=pl.BlockSpec(memory_space=pltpu.VMEM),
        out_shape=jax.ShapeDtypeStruct(parts.shape[1:], BF16),
        compiler_params=pltpu.CompilerParams(vmem_limit_bytes=VMEM),
    )(parts)


def attend_kernel(len_ref, m_ref, att_ref):
    rows = m_ref.shape[1] - 112
    half = rows // 2
    at = [rows + 32 * p for p in range(3)]
    stats = jnp.sum(m_ref[:, rows + 96 : rows + 112, :].astype(F32), axis=0)
    stats = jnp.concatenate(
        [stats[2 * p : 2 * p + 1] + stats[2 * p + 1 : 2 * p + 2] for p in range(3)], axis=1
    )
    scale = lax.rsqrt(stats * (1.0 / WIDTH) + EPS)
    wide = jnp.broadcast_to(scale, (HEAD, rows))
    key = jnp.concatenate([m_ref[:, a : a + 16, :].reshape(HEAD, 128) for a in at], axis=1)
    key = (key.astype(F32) * wide).astype(BF16)
    value = jnp.concatenate([m_ref[:, a + 16 : a + 32, :].reshape(HEAD, 128) for a in at], axis=1)
    value = (value.astype(F32) * wide).astype(BF16)
    column = wide.T[:, 0:1] * (1.0 / HEAD**0.5)
    for seq in range(2):
        first = seq * 128
        k = key[:, first : first + 256]
        v = value[:, first : first + 256]
        i = lax.broadcasted_iota(jnp.int32, (half, 256), 0)
        j = lax.broadcasted_iota(jnp.int32, (half, 256), 1) - (seq * half - first)
        allowed = (j >= 0) & (j <= i) & (j < len_ref[seq])
        c = column[seq * half : (seq + 1) * half]
        for head in range(NZ):
            q = m_ref[head, seq * half : (seq + 1) * half, :]
            scores = jnp.dot(q, k, preferred_element_type=F32) * c
            scores = jnp.where(allowed, scores, F32(-1e30))
            scores = scores - jnp.max(scores, axis=1, keepdims=True)
            expo = jnp.exp(scores)
            probs = (expo * (1.0 / jnp.sum(expo, axis=1, keepdims=True))).astype(BF16)
            o = lax.dot_general(probs, v, NT, preferred_element_type=F32)
            att_ref[seq * half : (seq + 1) * half, head * 128 : (head + 1) * 128] = o.astype(BF16)


def output_kernel(att_ref, w_ref, out_ref):
    a = att_ref[...]
    for d in range(2):
        for hi in range(2):
            w = jnp.concatenate(
                [w_ref[2 * k + d, hi * 128 : (hi + 1) * 128] for k in range(NZ)], axis=0
            )
            out_ref[2 * hi + d] = jnp.dot(a, w, preferred_element_type=F32).astype(BF16)


def attend(lengths, messages):
    rows = messages.shape[1] - 112
    vmem = pl.BlockSpec(memory_space=pltpu.VMEM)
    smem = pl.BlockSpec(memory_space=pltpu.SMEM)
    return pl.pallas_call(
        attend_kernel,
        in_specs=[smem, vmem],
        out_specs=vmem,
        out_shape=jax.ShapeDtypeStruct((rows, NZ * HEAD), BF16),
        compiler_params=pltpu.CompilerParams(vmem_limit_bytes=VMEM),
        cost_estimate=pl.CostEstimate(flops=ATTEND_COST, bytes_accessed=2_000_000, transcendentals=1_000_000),
    )(lengths, messages)


def output_products(attended, weights):
    rows = attended.shape[0]
    vmem = pl.BlockSpec(memory_space=pltpu.VMEM)
    return pl.pallas_call(
        output_kernel,
        in_specs=[vmem, vmem],
        out_specs=vmem,
        out_shape=jax.ShapeDtypeStruct((4, rows, 256), BF16),
        compiler_params=pltpu.CompilerParams(vmem_limit_bytes=VMEM),
        cost_estimate=pl.CostEstimate(flops=2 * rows * 1024 * 1024, bytes_accessed=5_000_000, transcendentals=0),
    )(attended, weights)


def resid_kernel(p_ref, x_ref, head_ref, resid_ref, stat_ref):
    update = jnp.sum(p_ref[...].astype(F32), axis=0)
    resid = (x_ref[...].astype(F32) + update).astype(BF16)
    resid_ref[...] = resid
    head = head_ref[...]
    h1 = head.astype(BF16)
    h2 = (head - h1.astype(F32)).astype(BF16)
    h3 = (head - h1.astype(F32) - h2.astype(F32)).astype(BF16)
    scores = sum(
        lax.dot_general(h, resid, NT, preferred_element_type=F32) for h in (h3, h2, h1)
    )
    row = lax.broadcasted_iota(jnp.int32, scores.shape, 0)
    stat = jnp.where(row < 6, scores, row_squares(resid)[0:8]).astype(BF16)
    for k in range(NZ * NYH):
        stat_ref[k] = stat


def resid_and_stats(parts, tokens, heads):
    rows, cols = tokens.shape
    return pl.pallas_call(
        resid_kernel,
        in_specs=[pl.BlockSpec(memory_space=pltpu.VMEM)] * 3,
        out_specs=[pl.BlockSpec(memory_space=pltpu.VMEM)] * 2,
        out_shape=[
            jax.ShapeDtypeStruct((rows, cols), BF16),
            jax.ShapeDtypeStruct((NZ * NYH, 8, rows), BF16),
        ],
        compiler_params=pltpu.CompilerParams(vmem_limit_bytes=VMEM),
        cost_estimate=pl.CostEstimate(flops=2 * rows * cols * 96, bytes_accessed=1_200_000, transcendentals=0),
    )(parts, tokens, heads)


def local(
    tokens,
    row_lengths,
    attn_gain,
    query_weight,
    key_weight,
    value_matrix,
    output_weight,
    final_gain,
    value_head,
):
    rows = tokens.shape[0]
    z, yh, c = lax.axis_index("z"), lax.axis_index("yh"), lax.axis_index("c")
    core = c.astype(jnp.int32)[None]

    xf = tokens.astype(F32)
    gained = (xf * attn_gain[None, :]).astype(BF16)

    first, even = (yh // 2) == 0, (yh % 2) == 0
    with jax.named_scope("weights_yh"):
        kv = lax.ppermute(jnp.concatenate([key_weight.T, value_matrix.T], axis=0), TP, kv_perm())
        q = [query_weight[256 * b : 256 * (b + 1)] for b in range(2)]
        q = [jnp.concatenate([one[:128], one[128:]], axis=1) for one in q]
        q = [
            lax.ppermute(jnp.where(first, q[k], q[1 - k]), ("yh", "c"), head_perm(k))
            for k in range(2)
        ]
        kv = [kv[:, :256], kv[:, 256:]]
        kv = [
            lax.ppermute(jnp.where(first, kv[k], kv[1 - k]), ("yh", "c"), head_perm(k))
            for k in range(2)
        ]
        odd = (yh % 2).astype(jnp.int32)[None]
        qkv_send = packed_copies(odd, *q, *kv)
    with jax.named_scope("out_yh"):
        o = [output_weight[:128], output_weight[128:]]
        o = [jnp.where(first, o[k], o[1 - k]) for k in range(2)]
        o, qkv_send = lax.optimization_barrier((o, qkv_send))
        o = [lax.ppermute(o[k], ("yh", "c"), head_perm(k)) for k in range(2)]


    swap = [(0, 1), (1, 0)]
    with jax.named_scope("tokens_z"):
        x_all = lax.all_gather(gained, "z", axis=0)
    with jax.named_scope("qkv_rep"):
        qkv_own = lax.all_to_all(qkv_send, ("yl", "x"), 0, 0)
        qkv_other = lax.ppermute(qkv_own, "c", swap)
    with jax.named_scope("out_rep"):
        o, x_all = lax.optimization_barrier((o, x_all))
        out_part = jnp.concatenate([jnp.where(even, o[k], o[1 - k]) for k in range(2)], axis=0)
        out_all = lax.all_gather(out_part, REP, axis=0)
    parts = project(core, x_all, qkv_own, qkv_other, tokens)
    with jax.named_scope("qkv_sum"):
        parts = lax.all_to_all(parts, "yh", 0, 0)
    with jax.named_scope("qkv_z"):
        messages = lax.all_gather(summed(parts), "z", axis=0)
    out_all, messages = lax.optimization_barrier((out_all, messages))
    attended = attend(row_lengths, messages)
    parts = output_products(attended, out_all)
    with jax.named_scope("out_sum"):
        parts = lax.all_to_all(parts, "yh", 0, 0)

    heads = jnp.concatenate([(final_gain[:, None] * value_head).T, jnp.zeros((2, tokens.shape[1]), F32)], axis=0)
    resid_out, stat = resid_and_stats(parts, tokens, heads)

    with jax.named_scope("stat_tp"):
        stat = lax.all_to_all(stat, TP, 0, 0).astype(F32).sum(axis=0)
    logits = stat[:6] * lax.rsqrt(stat[6] / WIDTH + EPS)[None, :]
    position = jnp.arange(rows // row_lengths.shape[0], dtype=jnp.int32)
    live = (position[None, :] < row_lengths[:, None]).reshape(1, rows)
    scores = jnp.where(live, logits, F32(0.0)).T
    return resid_out, scores


def solution(mesh):
    split = Mesh(mesh.devices.reshape(NZ, NYH, NYL, NX, NC), TP + REP)
    in_specs = (
        P(REP, TP),
        P(REP),
        P(TP),
        P(REP, TP),
        P(REP, TP),
        P(REP, TP),
        P(REP, TP),
        P(TP),
        P(TP, None),
    )
    out_specs = (P(REP, TP), P(REP, None))
    return jax.shard_map(local, mesh=split, in_specs=in_specs, out_specs=out_specs, check_vma=False)
```
